256 devices in a mesh: wide: 32 (over y, x, core), narrow: 8 (over z).
Axes of the slice: x: 4, y: 4, z: 8, core: 2. Of those that a mesh axis runs over, the one named last changes fastest.
Arguments:
- panel: float32 [64, 4194304], P(None, ('wide', 'narrow'))
- signs: int32 [4194304], P(('wide', 'narrow')), may hold values from -1 to 1, as said below
- sample_rows: int32 [16384], replicated, may hold values from 0 to 4194303, as said below
Outputs:
- mixed: float32 [64, 4194304], P(None, ('wide', 'narrow'))
- r_factor: float32 [64, 64], replicated
- precond: float32 [64, 4194304], P(None, ('wide', 'narrow'))
The draws below stay inside these ranges and needn't reach their ends.
Inputs may be any that keep to these rules, and one draw needn't show every extreme that they name: `signs`: each value is 1 or -1. `sample_rows`: increasing, all distinct.
All inputs are finite; a program needn't handle non-finite values.
Results may differ from the reference program's by a relative error of at most 0.00011.
Values sent between devices are 32-bit elements; how exact they have to be, the bound alone decides.
A program may use at most 64 MiB of HBM per device.

```python
import math
import jax
import jax.numpy as jnp
import numpy as np
from jax import lax

K = 64
ROWS_DEV = 16384
S = 16384
ROWS = 4194304


def draw_panel(key, part):
    key = jax.random.fold_in(key, 11)
    keys = jax.random.split(key, 3)
    row_scale = jnp.exp(jax.random.uniform(keys[1], (ROWS,), jnp.float32, 0.0, math.log(10.0)))
    col_scale = jnp.exp(jax.random.uniform(keys[2], (K, 1), jnp.float32, 0.0, math.log(10.0)))
    noise = jax.random.normal(keys[0], (K, ROWS), jnp.float32)
    values = noise * row_scale[None, :] * col_scale
    return values.astype(jnp.float32)


def draw_signs(key, part):
    key = jax.random.fold_in(key, 5)
    return (2 * jax.random.randint(key, (ROWS,), 0, 2) - 1).astype(jnp.int32)


def draw_sample_rows(key, part):
    key = jax.random.fold_in(key, 7)
    devs = ROWS // ROWS_DEV
    marks = np.arange(devs + 1, dtype=np.int64)
    starts = S * marks * (marks + devs - 2) // (2 * devs * (devs - 1))
    counts = jnp.asarray((starts[1:] - starts[:-1]).astype(np.int32))
    widest = min(ROWS_DEV, 3 * S // (2 * devs) + 2)
    keys = jax.random.split(key, devs)
    perms = jax.vmap(lambda one: jax.random.permutation(one, ROWS_DEV))(keys).astype(jnp.int32)
    picks = perms[:, :widest]
    device_ids = jnp.arange(devs, dtype=jnp.int32)
    targets = jnp.where(device_ids == devs - 1, ROWS_DEV - 1, 0).astype(jnp.int32)
    offsets = jnp.where((device_ids == 0) | (device_ids == devs - 1), targets - picks[:, 0], 0)
    picks = jnp.mod(picks + offsets[:, None], ROWS_DEV).astype(jnp.int32)
    slots = jnp.arange(widest, dtype=jnp.int32)[None, :]
    valid = slots < counts[:, None]
    picks = jnp.where(valid, picks, ROWS_DEV)
    picks = jnp.sort(picks, axis=1)
    rows = picks + (device_ids * ROWS_DEV)[:, None]
    places = jnp.asarray(starts[:-1].astype(np.int32))[:, None] + slots
    places = jnp.where(valid, places, S)
    result = jnp.zeros((S,), jnp.int32).at[places.reshape(-1)].set(rows.reshape(-1).astype(jnp.int32), mode='drop')
    return result


def setup_inputs(seed: int = 0) -> dict:
    key_list = jax.random.split(jax.random.key(seed), 4)
    panel = draw_panel(jax.random.fold_in(key_list[3], 71), 0)
    signs = draw_signs(jax.random.fold_in(key_list[3], 71), 0)
    sample_rows = draw_sample_rows(jax.random.fold_in(key_list[3], 71), 0)
    return {"panel": panel, "signs": signs, "sample_rows": sample_rows}


def hadamard_rows(values):
    cols, count = values.shape
    half = 1
    while half < count:
        blocks = values.reshape(cols, count // (2 * half), 2, half)
        first = blocks[:, :, 0, :]
        second = blocks[:, :, 1, :]
        values = jnp.stack([first + second, first - second], axis=2).reshape(cols, count)
        half = half * 2
    return values

def reference(panel, signs, sample_rows):
    signed = panel * signs.astype(jnp.float32)[None, :]
    mixed = hadamard_rows(signed) * (1.0 / math.sqrt(ROWS))
    sample = jnp.take(mixed, sample_rows, axis=1)
    gram = jnp.dot(sample.astype(jnp.float32), sample.T.astype(jnp.float32), precision=lax.Precision.HIGHEST, preferred_element_type=jnp.float32)
    gram = gram * (ROWS / S)
    lower = jnp.linalg.cholesky(gram)
    r_factor = lower.T * (1.0 / math.sqrt(ROWS))
    rinv = jax.scipy.linalg.solve_triangular(r_factor, jnp.eye(K, dtype=jnp.float32), lower=False)
    precond = jnp.dot(rinv.T.astype(jnp.float32), panel.astype(jnp.float32), precision=lax.Precision.HIGHEST, preferred_element_type=jnp.float32)
    return (mixed, r_factor, precond)
```

```python
import functools
import math

import jax
import jax.numpy as jnp
import numpy as np
from jax import lax
from jax.experimental import pallas as pl
from jax.experimental.pallas import tpu as pltpu
from jax.sharding import PartitionSpec as P

MESH = pl.DeviceIdType.MESH
F32 = jnp.float32
BF16 = jnp.bfloat16
NT = (((1,), (1,)), ((), ()))

N_Y, N_X, N_CORE, N_Z = 4, 4, 2, 8
PLANE = N_Y * N_X
COLS = 64
COUNT = 16384
GROUP = 8
CHUNKS = COLS // GROUP
HALF = CHUNKS // 2
Z_LEN = COUNT // N_Z
P_LEN = COUNT // PLANE
INNER = 256


def sylvester(order):
    matrix = np.ones((1, 1), np.float32)
    while matrix.shape[0] < order:
        matrix = np.block([[matrix, matrix], [matrix, -matrix]])
    return matrix


def butterflies(parts):
    parts = list(parts)
    half = 1
    while half < len(parts):
        for low in range(len(parts)):
            if not low & half:
                first, second = parts[low], parts[low | half]
                parts[low], parts[low | half] = first + second, first - second
        half *= 2
    return parts


def lanes(start, size):
    return pl.ds(pl.multiple_of(start, 128), size)


def device(y, x, core, z):
    return (((y % N_Y) * N_X + x % N_X) * N_CORE + core % N_CORE, z % N_Z)


def mix_kernel(
    panel_ref, signs_ref, samples_ref, h_ref, mixed_ref, gram_ref,
    panel, s0, r1, s1, r2, s2, r3, s3, r4, e, tw, weight, g_own, g_z, g_zsum, g_plane,
    in_sem, out_sem, send1, recv1, send2, recv2, send3, recv3, send4, recv4,
    send_core, recv_core, send_gz, recv_gz, send_gp, recv_gp, send_gg, recv_gg,
):
    wide = lax.axis_index("wide")
    z = lax.axis_index("narrow")
    core = wide % N_CORE
    x = (wide // N_CORE) % N_X
    y = wide // (N_CORE * N_X)
    q = wide // N_CORE
    z_peers = [device(y, x, core, z + d) for d in range(1, N_Z)]
    z_index = [(z + d) % N_Z for d in range(1, N_Z)]
    xy_offsets = [(a, b) for a in range(N_Y) for b in range(N_X) if a or b]
    xy_peers = [device(y + a, x + b, core, z) for a, b in xy_offsets]
    xy_index = [((y + a) % N_Y) * N_X + (x + b) % N_X for a, b in xy_offsets]
    sibling = device(y, x, core + 1, z)
    crossed = [device(y + a, x + b, core + 1, z) for a, b in xy_offsets]
    plane_peers = xy_peers + [sibling] + crossed

    def load(c):
        return pltpu.make_async_copy(
            panel_ref.at[pl.ds(pl.multiple_of(c * GROUP, GROUP), GROUP)], panel.at[c], in_sem.at[c]
        )

    for i in range(HALF):
        load(i).start()
        load(HALF + i).start()

    barrier = pltpu.get_barrier_semaphore()
    for peer in z_peers + plane_peers:
        pl.semaphore_signal(barrier, inc=1, device_id=peer, device_id_type=MESH)
    pl.semaphore_wait(barrier, len(z_peers) + len(plane_peers))

    def send(over_z, src, dst, c, send_sem, recv_sem):
        size = Z_LEN if over_z else P_LEN
        mine = (z if over_z else q) * size
        peers, index = (z_peers, z_index) if over_z else (xy_peers, xy_index)
        for peer, place in zip(peers, index):
            pltpu.make_async_remote_copy(
                src_ref=src.at[c, :, lanes(place * size, size)],
                dst_ref=dst.at[c, :, lanes(mine, size)],
                send_sem=send_sem.at[c],
                recv_sem=recv_sem.at[c],
                device_id=peer,
                device_id_type=MESH,
            ).start()

    def await_bytes(over_z, ref, c, sem):
        part = ref.at[c, :, pl.ds(0, COUNT - (Z_LEN if over_z else P_LEN))]
        pltpu.make_async_copy(part, part, sem.at[c]).wait()

    def combine(over_z, own, got, out, back, c):
        size = Z_LEN if over_z else P_LEN
        n = N_Z if over_z else PLANE
        mine = lanes((z if over_z else q) * size, size)
        got[c, :, mine] = own[c, :, mine]
        step = 4096 // n

        def part(i, carry):
            places = [lanes(p * size + i * step, step) for p in range(n)]
            values = butterflies([got[c, :, place] for place in places])
            for place, value in zip(places, values):
                out[c, :, place] = value
            return carry

        lax.fori_loop(0, size // step, part, 0)
        back[c, :, mine] = out[c, :, mine]

    def core_copy(c):
        return pltpu.make_async_remote_copy(
            src_ref=r2.at[c], dst_ref=e.at[c], send_sem=send_core.at[c], recv_sem=recv_core.at[c],
            device_id=sibling, device_id_type=MESH,
        )

    flip = 1.0 - 2.0 * core.astype(F32)

    def core_combine(c):
        core_copy(c).start()
        core_copy(c).wait_recv()

        def part(i, carry):
            place = lanes(i * 2048, 2048)
            s2[c, :, place] = e[c, :, place] + flip * r2[c, :, place]
            return carry

        lax.fori_loop(0, COUNT // 2048, part, 0)

    def mix(c):
        load(c).wait()

        def slab(i, carry):
            place = lanes(i * 1024, 1024)
            values = panel[c, :, place] * signs_ref[:, place].astype(F32)
            low = values - values.astype(BF16).astype(F32)
            rows = []
            for b in range(1024 // INNER):
                rows += [values[:, b * INNER:(b + 1) * INNER], low[:, b * INNER:(b + 1) * INNER]]
            stacked = jnp.concatenate(rows, axis=0).astype(BF16)
            done = jnp.dot(stacked, h_ref[...], preferred_element_type=F32)
            parts = [
                done[16 * b:16 * b + 8] + done[16 * b + 8:16 * b + 16] for b in range(1024 // INNER)
            ]
            s0[c, :, place] = jnp.concatenate(butterflies(parts), axis=1)
            return carry

        lax.fori_loop(0, COUNT // 1024, slab, 0)

        def part(i, carry):
            places = [lanes(p * 1024 + i * 256, 256) for p in range(16)]
            values = butterflies([s0[c, :, place] for place in places])
            for place, value in zip(places, values):
                s0[c, :, place] = value
            return carry

        lax.fori_loop(0, 4, part, 0)

    def begin(i, carry):
        mix(i)
        send(True, s0, r1, i, send1, recv1)
        mix(HALF + i)
        send(False, s0, r1, HALF + i, send1, recv1)
        return carry

    lax.fori_loop(0, HALF, begin, 0)

    base = (wide * N_Z + z) * COUNT
    weight[...] = jnp.zeros_like(weight)

    def mark(i, carry):
        offsets = samples_ref[pl.ds(i * 8, 8), :] - base
        high = jnp.right_shift(offsets, 7)
        low = jnp.bitwise_and(offsets, 127)
        places = lax.broadcasted_iota(jnp.int32, (128, 128), 0)
        total = jnp.zeros((128, 128), F32)
        for r in range(0, 8, 2):
            above = [jnp.where(places == high[k:k + 1], 1.0, 0.0) for k in (r, r + 1)]
            below = [jnp.where(places == low[k:k + 1], 1.0, 0.0) for k in (r, r + 1)]
            total += lax.dot_general(
                jnp.concatenate(above, axis=1).astype(BF16),
                jnp.concatenate(below, axis=1).astype(BF16),
                NT,
                preferred_element_type=F32,
            )
        weight[...] += total
        return carry

    lax.fori_loop(0, 16, mark, 0)

    def second(i, carry):
        b = HALF + i
        await_bytes(False, r1, b, recv1)
        combine(False, s0, r1, s1, r2, b)
        send(False, s1, r2, b, send2, recv2)
        await_bytes(True, r1, i, recv1)
        combine(True, s0, r1, s1, r2, i)
        send(True, s1, r2, i, send2, recv2)
        return carry

    lax.fori_loop(0, HALF, second, 0)

    def third(i, carry):
        b = HALF + i
        await_bytes(False, r2, b, recv2)
        core_combine(b)
        send(True, s2, r3, b, send3, recv3)
        return carry

    lax.fori_loop(0, HALF, third, 0)

    def fourth(i, carry):
        await_bytes(True, r2, i, recv2)
        core_combine(i)
        send(False, s2, r3, i, send3, recv3)
        return carry

    lax.fori_loop(0, HALF, fourth, 0)

    def fifth(i, carry):
        await_bytes(False, r3, i, recv3)
        combine(False, s2, r3, s3, r4, i)
        send(False, s3, r4, i, send4, recv4)
        return carry

    lax.fori_loop(0, HALF, fifth, 0)

    def store(c):
        return pltpu.make_async_copy(
            r4.at[c], mixed_ref.at[pl.ds(pl.multiple_of(c * GROUP, GROUP), GROUP)], out_sem.at[c]
        )

    def final(c):
        store(c).start()

        def slab(i, carry):
            place = lanes(i * 1024, 1024)
            rows = weight[pl.ds(pl.multiple_of(i * 8, 8), 8), :]
            mask = jnp.concatenate([rows[k:k + 1] for k in range(8)], axis=1)
            values = r4[c, :, place] * mask
            low = values - values.astype(BF16).astype(F32)
            both = jnp.concatenate([values, low], axis=0).astype(BF16)
            tw[pl.ds(pl.multiple_of(c * 16, 16), 16), place] = both
            return carry

        lax.fori_loop(0, COUNT // 1024, slab, 0)

    def sixth(i, carry):
        b = HALF + i
        await_bytes(True, r3, b, recv3)
        combine(True, s2, r3, s3, r4, b)
        send(True, s3, r4, b, send4, recv4)
        await_bytes(False, r4, i, recv4)
        final(i)
        return carry

    lax.fori_loop(0, HALF, sixth, 0)

    def seventh(i, carry):
        b = HALF + i
        await_bytes(True, r4, b, recv4)
        final(b)
        return carry

    lax.fori_loop(0, HALF, seventh, 0)

    def product(i, total):
        part = tw[:, lanes(i * 2048, 2048)]
        return total + lax.dot_general(part, part, NT, preferred_element_type=F32)

    total = lax.fori_loop(0, COUNT // 2048, product, jnp.zeros((128, 128), F32))
    rows = jnp.concatenate(
        [total[16 * c:16 * c + 8] + total[16 * c + 8:16 * c + 16] for c in range(CHUNKS)], axis=0
    )
    lane = lax.broadcasted_iota(jnp.int32, (128, 128), 0)
    column = lax.broadcasted_iota(jnp.int32, (128, 128), 1)
    chosen = jnp.where((lane // 16) * 8 + lane % 8 == column, 1.0, 0.0)
    g_own[...] = jnp.dot(rows, chosen, precision=lax.Precision.HIGHEST, preferred_element_type=F32)

    def rows_of(place):
        return pl.ds(pl.multiple_of(place * GROUP, GROUP), GROUP)

    for peer, place in zip(z_peers, z_index):
        pltpu.make_async_remote_copy(
            src_ref=g_own.at[rows_of(place)], dst_ref=g_z.at[z], send_sem=send_gz.at[0],
            recv_sem=recv_gz.at[0], device_id=peer, device_id_type=MESH,
        ).start()
    g_z[z] = g_own[rows_of(z)]
    others = g_z.at[pl.ds(0, N_Z - 1)]
    pltpu.make_async_copy(others, others, recv_gz.at[0]).wait()
    g_zsum[...] = functools.reduce(lambda a, b: a + b, [g_z[k] for k in range(N_Z)])
    for peer in plane_peers:
        pltpu.make_async_remote_copy(
            src_ref=g_zsum, dst_ref=g_plane.at[wide], send_sem=send_gp.at[0],
            recv_sem=recv_gp.at[0], device_id=peer, device_id_type=MESH,
        ).start()
    g_plane[wide] = g_zsum[...]
    planes = g_plane.at[pl.ds(0, PLANE * N_CORE - 1)]
    pltpu.make_async_copy(planes, planes, recv_gp.at[0]).wait()
    gram_ref[rows_of(z)] = functools.reduce(
        lambda a, b: a + b, [g_plane[k] for k in range(PLANE * N_CORE)]
    )
    for peer in z_peers:
        pltpu.make_async_remote_copy(
            src_ref=gram_ref.at[rows_of(z)], dst_ref=gram_ref.at[rows_of(z)], send_sem=send_gg.at[0],
            recv_sem=recv_gg.at[0], device_id=peer, device_id_type=MESH,
        ).start()
    bands = gram_ref.at[pl.ds(0, COLS - GROUP)]
    pltpu.make_async_copy(bands, bands, recv_gg.at[0]).wait()

    pltpu.make_async_copy(others, others, send_gz.at[0]).wait()
    pltpu.make_async_copy(planes, planes, send_gp.at[0]).wait()
    pltpu.make_async_copy(bands, bands, send_gg.at[0]).wait()

    def drain(i, carry):
        b = HALF + i
        await_bytes(True, s0, i, send1)
        await_bytes(False, s0, b, send1)
        await_bytes(True, s1, i, send2)
        await_bytes(False, s1, b, send2)
        await_bytes(False, s2, i, send3)
        await_bytes(True, s2, b, send3)
        await_bytes(False, s3, i, send4)
        await_bytes(True, s3, b, send4)
        core_copy(i).wait_send()
        core_copy(b).wait_send()
        store(i).wait()
        store(b).wait()
        return carry

    lax.fori_loop(0, HALF, drain, 0)


def finish_kernel(
    scale, root, gram_ref, panel_ref, mixed_in, mixed_ref, r_ref, precond_ref,
    panel, out, mixed_sem, in_sem, out_sem,
):
    copy_mixed = pltpu.make_async_copy(mixed_in, mixed_ref, mixed_sem)
    copy_mixed.start()
    copy_panel = pltpu.make_async_copy(panel_ref, panel, in_sem)
    copy_panel.start()
    row = lax.broadcasted_iota(jnp.int32, (COLS, 2 * COLS), 0)
    column = lax.broadcasted_iota(jnp.int32, (COLS, 2 * COLS), 1)
    start = jnp.where(
        column < COLS, gram_ref[...] * scale, jnp.where(column - COLS == row, 1.0, 0.0)
    )
    bands = [start[8 * b:8 * b + 8] for b in range(COLS // 8)]
    sub = lax.broadcasted_iota(jnp.int32, (8, 1), 0)
    roots = []
    for k in range(COLS):
        home = k // 8
        line = bands[home][k % 8:k % 8 + 1]
        pivot = line[:, k:k + 1]
        roots.append(pivot)
        scaled = line / pivot
        for b in range(home, COLS // 8):
            factor = bands[b][:, k:k + 1]
            if b == home:
                factor = jnp.where(sub > k % 8, factor, 0.0)
            bands[b] = bands[b] - factor * scaled
    done = jnp.concatenate(bands, axis=0)
    diagonal = jnp.sqrt(jnp.concatenate(roots, axis=0))
    done = done / diagonal
    square = done[:, :COLS]
    upper = lax.broadcasted_iota(jnp.int32, (COLS, COLS), 1) >= lax.broadcasted_iota(
        jnp.int32, (COLS, COLS), 0
    )
    r_ref[...] = jnp.where(upper, square * (1.0 / root), 0.0)
    inverse = done[:, COLS:] * root
    high = inverse.astype(BF16)
    low = (inverse - high.astype(F32)).astype(BF16)
    left = jnp.concatenate([high, low, high], axis=1)

    copy_panel.wait()

    def tile(i):
        place = lanes(i * 1024, 1024)
        return pltpu.make_async_copy(out.at[:, place], precond_ref.at[:, place], out_sem.at[i])

    def multiply(i, carry):
        place = lanes(i * 1024, 1024)
        values = panel[:, place]
        values_high = values.astype(BF16)
        values_low = (values - values_high.astype(F32)).astype(BF16)
        right = jnp.concatenate([values_high, values_high, values_low], axis=0)
        out[:, place] = jnp.dot(left, right, preferred_element_type=F32)
        tile(i).start()
        return carry

    lax.fori_loop(0, COUNT // 1024, multiply, 0)

    def drain(i, carry):
        tile(i).wait()
        return carry

    lax.fori_loop(0, COUNT // 1024, drain, 0)
    copy_mixed.wait()


def body(panel, signs, sample_rows):
    cols, count = panel.shape
    total = count * lax.axis_size("wide") * lax.axis_size("narrow")
    root = math.sqrt(total)
    any_space = pl.BlockSpec(memory_space=pl.ANY)
    vmem = pl.BlockSpec(memory_space=pltpu.VMEM)
    mixer = jnp.asarray(sylvester(INNER) / root, BF16)
    chunked = pltpu.VMEM((CHUNKS, GROUP, count), F32)
    dma = pltpu.SemaphoreType.DMA
    mixed, gram = pl.pallas_call(
        mix_kernel,
        out_shape=(
            jax.ShapeDtypeStruct((cols, count), F32),
            jax.ShapeDtypeStruct((cols, 128), F32),
        ),
        in_specs=[any_space, vmem, vmem, vmem],
        out_specs=(any_space, vmem),
        scratch_shapes=[chunked] * 10
        + [
            pltpu.VMEM((2 * cols, count), BF16),
            pltpu.VMEM((128, 128), F32),
            pltpu.VMEM((cols, 128), F32),
            pltpu.VMEM((N_Z, GROUP, 128), F32),
            pltpu.VMEM((GROUP, 128), F32),
            pltpu.VMEM((PLANE * N_CORE, GROUP, 128), F32),
        ]
        + [dma((CHUNKS,))] * 12
        + [dma((1,))] * 6,
        compiler_params=pltpu.CompilerParams(
            collective_id=0, has_side_effects=True, vmem_limit_bytes=56 * 1024 * 1024
        ),
    )(panel, signs.reshape(1, count), sample_rows.reshape(-1, 128), mixer)
    mixed, r_factor, precond = pl.pallas_call(
        functools.partial(finish_kernel, total / sample_rows.shape[0], root),
        out_shape=(
            jax.ShapeDtypeStruct((cols, count), F32),
            jax.ShapeDtypeStruct((cols, cols), F32),
            jax.ShapeDtypeStruct((cols, count), F32),
        ),
        in_specs=[vmem, any_space, any_space],
        out_specs=(any_space, vmem, any_space),
        scratch_shapes=[
            pltpu.VMEM((cols, count), F32),
            pltpu.VMEM((cols, count), F32),
            dma,
            dma,
            dma((count // 1024,)),
        ],
        compiler_params=pltpu.CompilerParams(vmem_limit_bytes=40 * 1024 * 1024),
    )(gram, panel, mixed)
    return (mixed, r_factor, precond)


def solution(mesh):
    in_specs = (P(None, ("wide", "narrow")), P(("wide", "narrow")), P())
    out_specs = (P(None, ("wide", "narrow")), P(), P(None, ("wide", "narrow")))
    return jax.shard_map(body, mesh=mesh, in_specs=in_specs, out_specs=out_specs, check_vma=False)
```

```python
import functools
import math

import jax
import jax.numpy as jnp
import numpy as np
from jax import lax
from jax.experimental import pallas as pl
from jax.experimental.pallas import tpu as pltpu
from jax.sharding import PartitionSpec as P

MESH = pl.DeviceIdType.MESH
F32 = jnp.float32
BF16 = jnp.bfloat16
NT = (((1,), (1,)), ((), ()))

N_Y, N_X, N_CORE, N_Z = 4, 4, 2, 8
PLANE = N_Y * N_X
COLS = 64
COUNT = 16384
GROUP = 8
CHUNKS = COLS // GROUP
AHEAD = 4
Z_LEN = COUNT // N_Z
P_LEN = COUNT // PLANE
INNER = 256


def sylvester(order):
    matrix = np.ones((1, 1), np.float32)
    while matrix.shape[0] < order:
        matrix = np.block([[matrix, matrix], [matrix, -matrix]])
    return matrix


def butterflies(parts):
    parts = list(parts)
    half = 1
    while half < len(parts):
        for low in range(len(parts)):
            if not low & half:
                first, second = parts[low], parts[low | half]
                parts[low], parts[low | half] = first + second, first - second
        half *= 2
    return parts


def lanes(start, size):
    return pl.ds(pl.multiple_of(start, 128), size)


def device(y, x, core, z):
    return (((y % N_Y) * N_X + x % N_X) * N_CORE + core % N_CORE, z % N_Z)


def mix_kernel(
    scale, root, panel_ref, signs_ref, samples_ref, h_ref, mixed_ref, r_ref, precond_ref,
    panel, s0, r1, s1, r2, s2, r3, e, s3, out, tw, weight, g_own, g_z, g_zsum, g_plane, gram,
    in_sem, own_sem, out_sem, send1, recv1, send2, recv2, send3, recv3, send4, recv4,
    send_core, recv_core, send_gz, recv_gz, send_gp, recv_gp, send_gg, recv_gg,
):
    wide = lax.axis_index("wide")
    z = lax.axis_index("narrow")
    core = wide % N_CORE
    x = (wide // N_CORE) % N_X
    y = wide // (N_CORE * N_X)
    q = wide // N_CORE
    z_peers = [device(y, x, core, z + d) for d in range(1, N_Z)]
    z_index = [(z + d) % N_Z for d in range(1, N_Z)]
    xy_offsets = [(a, b) for a in range(N_Y) for b in range(N_X) if a or b]
    xy_peers = [device(y + a, x + b, core, z) for a, b in xy_offsets]
    xy_index = [((y + a) % N_Y) * N_X + (x + b) % N_X for a, b in xy_offsets]
    sibling = device(y, x, core + 1, z)
    crossed = [device(y + a, x + b, core + 1, z) for a, b in xy_offsets]
    plane_peers = xy_peers + [sibling] + crossed

    def band(c):
        return pl.ds(pl.multiple_of(c * GROUP, GROUP), GROUP)

    def load(c):
        return pltpu.make_async_copy(panel_ref.at[band(c)], panel.at[c], in_sem.at[c])

    for c in range(CHUNKS):
        load(c).start()

    barrier = pltpu.get_barrier_semaphore()
    for peer in z_peers + plane_peers:
        pl.semaphore_signal(barrier, inc=1, device_id=peer, device_id_type=MESH)

    def send(over_z, src, target, c, send_sem, recv_sem):
        size = Z_LEN if over_z else P_LEN
        peers, index = (z_peers, z_index) if over_z else (xy_peers, xy_index)
        for peer, place in zip(peers, index):
            pltpu.make_async_remote_copy(
                src_ref=src.at[c, :, lanes(place * size, size)],
                dst_ref=target(lanes((z if over_z else q) * size, size)),
                send_sem=send_sem.at[c],
                recv_sem=recv_sem.at[c],
                device_id=peer,
                device_id_type=MESH,
            ).start()

    def await_bytes(over_z, ref, c, sem):
        part = ref.at[c, :, pl.ds(0, COUNT - (Z_LEN if over_z else P_LEN))]
        pltpu.make_async_copy(part, part, sem.at[c]).wait()

    def combine(over_z, own, got, out, c):
        size = Z_LEN if over_z else P_LEN
        n = N_Z if over_z else PLANE
        mine = lanes((z if over_z else q) * size, size)
        got[c, :, mine] = own[c, :, mine]
        step = 4096 // n

        def part(i, carry):
            places = [lanes(p * size + i * step, step) for p in range(n)]
            values = butterflies([got[c, :, place] for place in places])
            for place, value in zip(places, values):
                out[c, :, place] = value
            return carry

        lax.fori_loop(0, size // step, part, 0)

    def mix(c):
        load(c).wait()

        def slab(i, carry):
            place = lanes(i * 1024, 1024)
            values = panel[c, :, place] * signs_ref[:, place].astype(F32)
            low = values - values.astype(BF16).astype(F32)
            rows = []
            for b in range(1024 // INNER):
                rows += [values[:, b * INNER:(b + 1) * INNER], low[:, b * INNER:(b + 1) * INNER]]
            stacked = jnp.concatenate(rows, axis=0).astype(BF16)
            done = jnp.dot(stacked, h_ref[...], preferred_element_type=F32)
            parts = [
                done[16 * b:16 * b + 8] + done[16 * b + 8:16 * b + 16] for b in range(1024 // INNER)
            ]
            s0[c, :, place] = jnp.concatenate(butterflies(parts), axis=1)
            return carry

        lax.fori_loop(0, COUNT // 1024, slab, 0)

        def part(i, carry):
            places = [lanes(p * 1024 + i * 256, 256) for p in range(16)]
            values = butterflies([s0[c, :, place] for place in places])
            for place, value in zip(places, values):
                s0[c, :, place] = value
            return carry

        lax.fori_loop(0, 4, part, 0)

    def send_z(c):
        send(True, s0, lambda place: r1.at[c, :, place], c, send1, recv1)

    mix(0)
    pl.semaphore_wait(barrier, len(z_peers) + len(plane_peers))
    send_z(0)

    def begin(c, carry):
        mix(c)
        send_z(c)
        return carry

    lax.fori_loop(1, CHUNKS, begin, 0)

    weight[...] = jnp.zeros_like(weight)

    def mark(i, carry):
        rows = samples_ref[pl.ds(pl.multiple_of(i * 8, 8), 8), :]
        offsets = rows - wide * (N_Z * COUNT)
        place = jnp.bitwise_and(jnp.right_shift(offsets, 11), N_Z - 1)
        inside = (jnp.right_shift(offsets, 17) == 0) & (place == z)
        inner = jnp.bitwise_and(jnp.right_shift(offsets, 7), Z_LEN // 128 - 1)
        high = jnp.where(inside, jnp.right_shift(offsets, 14) * (Z_LEN // 128) + inner, -1)
        low = jnp.bitwise_and(offsets, 127)
        places = lax.broadcasted_iota(jnp.int32, (128, 128), 0)
        total = jnp.zeros((128, 128), F32)
        for r in range(0, 8, 2):
            above = [jnp.where(places == high[k:k + 1], 1.0, 0.0) for k in (r, r + 1)]
            below = [jnp.where(places == low[k:k + 1], 1.0, 0.0) for k in (r, r + 1)]
            total += lax.dot_general(
                jnp.concatenate(above, axis=1).astype(BF16),
                jnp.concatenate(below, axis=1).astype(BF16),
                NT,
                preferred_element_type=F32,
            )
        weight[...] += total
        return carry

    lax.fori_loop(0, 16, mark, 0)

    def plane_out(c):
        await_bytes(True, r1, c, recv1)
        combine(True, s0, r1, s1, c)
        send(False, s1, lambda place: r2.at[c, :, place], c, send2, recv2)

    def plane_back(c):
        await_bytes(False, r2, c, recv2)
        combine(False, s1, r2, s2, c)
        send(False, s2, lambda place: r3.at[c, :, place], c, send3, recv3)

    def core_copy(c):
        return pltpu.make_async_remote_copy(
            src_ref=r3.at[c], dst_ref=e.at[c], send_sem=send_core.at[c], recv_sem=recv_core.at[c],
            device_id=sibling, device_id_type=MESH,
        )

    def core_out(c):
        await_bytes(False, r3, c, recv3)
        mine = lanes(q * P_LEN, P_LEN)
        r3[c, :, mine] = s2[c, :, mine]
        core_copy(c).start()

    flip = 1.0 - 2.0 * core.astype(F32)

    def keep(c):
        mine = lanes(z * Z_LEN, Z_LEN)
        return pltpu.make_async_copy(s3.at[c, :, mine], mixed_ref.at[band(c), mine], own_sem.at[c])

    def last(c):
        core_copy(c).wait_recv()

        def slab(i, carry):
            place = lanes(i * 1024, 1024)
            values = e[c, :, place] + flip * r3[c, :, place]
            s3[c, :, place] = values
            rows = weight[pl.ds(pl.multiple_of(i * 8, 8), 8), :]
            mask = jnp.concatenate([rows[k:k + 1] for k in range(8)], axis=1)
            values = values * mask
            low = values - values.astype(BF16).astype(F32)
            both = jnp.concatenate([values, low], axis=0).astype(BF16)
            tw[pl.ds(pl.multiple_of(c * 16, 16), 16), place] = both
            return carry

        lax.fori_loop(0, COUNT // 1024, slab, 0)
        keep(c).start()

    def z_back(c, carry):
        send(True, s3, lambda place: mixed_ref.at[band(c), place], c, send4, recv4)
        return carry

    def step(c, carry):
        plane_out(c)
        plane_back(c - 1)
        core_out(c - 2)
        last(c - 2)
        return carry

    def early(c, carry):
        step(c, carry)
        z_back(c - 2, carry)
        return carry

    plane_out(0)
    plane_out(1)
    plane_back(0)
    lax.fori_loop(2, AHEAD + 2, early, 0)
    lax.fori_loop(AHEAD + 2, CHUNKS, step, 0)
    plane_back(CHUNKS - 1)
    core_out(CHUNKS - 2)
    last(CHUNKS - 2)
    core_out(CHUNKS - 1)
    last(CHUNKS - 1)

    def product(i, total):
        part = tw[:, lanes(i * 2048, 2048)]
        return total + lax.dot_general(part, part, NT, preferred_element_type=F32)

    total = lax.fori_loop(0, COUNT // 2048, product, jnp.zeros((128, 128), F32))
    rows = jnp.concatenate(
        [total[16 * c:16 * c + 8] + total[16 * c + 8:16 * c + 16] for c in range(CHUNKS)], axis=0
    )
    lane = lax.broadcasted_iota(jnp.int32, (128, 128), 0)
    column = lax.broadcasted_iota(jnp.int32, (128, 128), 1)
    chosen = jnp.where((lane // 16) * 8 + lane % 8 == column, 1.0, 0.0)
    g_own[...] = jnp.dot(rows, chosen, precision=lax.Precision.HIGHEST, preferred_element_type=F32)

    for peer, place in zip(z_peers, z_index):
        pltpu.make_async_remote_copy(
            src_ref=g_own.at[band(place)], dst_ref=g_z.at[z], send_sem=send_gz.at[0],
            recv_sem=recv_gz.at[0], device_id=peer, device_id_type=MESH,
        ).start()
    z_back(AHEAD, 0)
    g_z[z] = g_own[band(z)]
    others = g_z.at[pl.ds(0, N_Z - 1)]
    pltpu.make_async_copy(others, others, recv_gz.at[0]).wait()
    g_zsum[...] = functools.reduce(lambda a, b: a + b, [g_z[k] for k in range(N_Z)])
    for peer in plane_peers:
        pltpu.make_async_remote_copy(
            src_ref=g_zsum, dst_ref=g_plane.at[wide], send_sem=send_gp.at[0],
            recv_sem=recv_gp.at[0], device_id=peer, device_id_type=MESH,
        ).start()
    g_plane[wide] = g_zsum[...]
    planes = g_plane.at[pl.ds(0, PLANE * N_CORE - 1)]
    pltpu.make_async_copy(planes, planes, recv_gp.at[0]).wait()
    gram[band(z)] = functools.reduce(
        lambda a, b: a + b, [g_plane[k] for k in range(PLANE * N_CORE)]
    )
    for peer in z_peers:
        pltpu.make_async_remote_copy(
            src_ref=gram.at[band(z)], dst_ref=gram.at[band(z)], send_sem=send_gg.at[0],
            recv_sem=recv_gg.at[0], device_id=peer, device_id_type=MESH,
        ).start()
    lax.fori_loop(AHEAD + 1, CHUNKS, z_back, 0)
    bands = gram.at[pl.ds(0, COLS - GROUP)]
    pltpu.make_async_copy(bands, bands, recv_gg.at[0]).wait()

    row = lax.broadcasted_iota(jnp.int32, (COLS, 2 * COLS), 0)
    column = lax.broadcasted_iota(jnp.int32, (COLS, 2 * COLS), 1)
    start = jnp.where(
        column < COLS, gram[...] * scale, jnp.where(column - COLS == row, 1.0, 0.0)
    )

    def eliminate(k, values):
        line = jnp.sum(jnp.where(row == k, values, 0.0), axis=0, keepdims=True)
        factor = jnp.sum(jnp.where((column == k) & (row > k), values, 0.0), axis=1, keepdims=True)
        pivot = jnp.sum(jnp.where(column[:1] == k, line, 0.0), axis=1, keepdims=True)
        return values - factor * (line / pivot)

    done = lax.fori_loop(0, COLS, eliminate, start)
    diagonal = jnp.sum(jnp.where(row == column, done, 0.0), axis=1, keepdims=True)
    done = done / jnp.sqrt(diagonal)
    square = done[:, :COLS]
    r_ref[...] = jnp.where(row[:, :COLS] <= column[:, :COLS], square * (1.0 / root), 0.0)
    inverse = done[:, COLS:] * root
    high = inverse.astype(BF16)
    low = (inverse - high.astype(F32)).astype(BF16)
    left = jnp.concatenate([high, low, high], axis=1)

    def tile(i):
        place = lanes(i * 1024, 1024)
        return pltpu.make_async_copy(out.at[:, place], precond_ref.at[:, place], out_sem.at[i])

    def multiply(i, carry):
        place = lanes(i * 1024, 1024)
        values = jnp.concatenate([panel[c, :, place] for c in range(CHUNKS)], axis=0)
        values_high = values.astype(BF16)
        values_low = (values - values_high.astype(F32)).astype(BF16)
        right = jnp.concatenate([values_high, values_high, values_low], axis=0)
        out[:, place] = jnp.dot(left, right, preferred_element_type=F32)
        tile(i).start()
        return carry

    lax.fori_loop(0, COUNT // 1024, multiply, 0)

    pltpu.make_async_copy(others, others, send_gz.at[0]).wait()
    pltpu.make_async_copy(planes, planes, send_gp.at[0]).wait()
    pltpu.make_async_copy(bands, bands, send_gg.at[0]).wait()

    def drain(i, carry):
        tile(i).wait()
        return carry

    lax.fori_loop(0, COUNT // 1024, drain, 0)

    def arrived(c, carry):
        await_bytes(True, s0, c, send1)
        await_bytes(False, s1, c, send2)
        await_bytes(False, s2, c, send3)
        core_copy(c).wait_send()
        keep(c).wait()
        await_bytes(True, s3, c, send4)
        part = mixed_ref.at[band(c), pl.ds(0, COUNT - Z_LEN)]
        pltpu.make_async_copy(part, part, recv4.at[c]).wait()
        return carry

    lax.fori_loop(0, CHUNKS, arrived, 0)


def body(panel, signs, sample_rows):
    cols, count = panel.shape
    total = count * lax.axis_size("wide") * lax.axis_size("narrow")
    root = math.sqrt(total)
    any_space = pl.BlockSpec(memory_space=pl.ANY)
    vmem = pl.BlockSpec(memory_space=pltpu.VMEM)
    mixer = jnp.asarray(sylvester(INNER) / root, BF16)
    chunked = pltpu.VMEM((CHUNKS, GROUP, count), F32)
    dma = pltpu.SemaphoreType.DMA
    return pl.pallas_call(
        functools.partial(mix_kernel, total / sample_rows.shape[0], root),
        out_shape=(
            jax.ShapeDtypeStruct((cols, count), F32),
            jax.ShapeDtypeStruct((cols, cols), F32),
            jax.ShapeDtypeStruct((cols, count), F32),
        ),
        in_specs=[any_space, vmem, vmem, vmem],
        out_specs=(any_space, vmem, any_space),
        scratch_shapes=[chunked] * 9
        + [
            pltpu.VMEM((cols, count), F32),
            pltpu.VMEM((2 * cols, count), BF16),
            pltpu.VMEM((128, 128), F32),
            pltpu.VMEM((cols, 128), F32),
            pltpu.VMEM((N_Z, GROUP, 128), F32),
            pltpu.VMEM((GROUP, 128), F32),
            pltpu.VMEM((PLANE * N_CORE, GROUP, 128), F32),
            pltpu.VMEM((cols, 128), F32),
        ]
        + [dma((CHUNKS,))] * 2
        + [dma((count // 1024,))]
        + [dma((CHUNKS,))] * 10
        + [dma((1,))] * 6,
        compiler_params=pltpu.CompilerParams(
            collective_id=0, has_side_effects=True, vmem_limit_bytes=56 * 1024 * 1024
        ),
    )(panel, signs.reshape(1, count), sample_rows.reshape(-1, 128), mixer)


def solution(mesh):
    in_specs = (P(None, ("wide", "narrow")), P(("wide", "narrow")), P())
    out_specs = (P(None, ("wide", "narrow")), P(), P(None, ("wide", "narrow")))
    return jax.shard_map(body, mesh=mesh, in_specs=in_specs, out_specs=out_specs, check_vma=False)
```

```python
import functools
import math

import jax
import jax.numpy as jnp
from jax import lax
from jax.experimental import pallas as pl
from jax.experimental.pallas import tpu as pltpu
from jax.sharding import PartitionSpec as P

MESH = pl.DeviceIdType.MESH
F32 = jnp.float32
BF16 = jnp.bfloat16
NT = (((1,), (1,)), ((), ()))

N_Y, N_X, N_CORE, N_Z = 4, 4, 2, 8
PLANE = N_Y * N_X
COLS = 64
COUNT = 16384
GROUP = 8
CHUNKS = COLS // GROUP
AHEAD = 4
Z_LEN = COUNT // N_Z
P_LEN = COUNT // PLANE
INNER = 256


def butterflies(parts):
    parts = list(parts)
    half = 1
    while half < len(parts):
        for low in range(len(parts)):
            if not low & half:
                first, second = parts[low], parts[low | half]
                parts[low], parts[low | half] = first + second, first - second
        half *= 2
    return parts


def lanes(start, size):
    return pl.ds(pl.multiple_of(start, 128), size)


def device(y, x, core, z):
    return (((y % N_Y) * N_X + x % N_X) * N_CORE + core % N_CORE, z % N_Z)


def mix_kernel(
    scale, root, panel_ref, signs_hbm, samples_hbm, mixed_ref, r_ref, out,
    panel, signs_ref, samples_ref, h_ref, s0, r1, s1, r2, s2, r3, e, s3, tw, weight,
    g_own, g_z, g_zsum, g_plane, g_psum, g_core, gram,
    in_sem, own_sem, signs_sem, samples_sem, send1, recv1, send2, recv2, send3, recv3, send4, recv4,
    send_core, recv_core, send_gz, recv_gz, send_gp, recv_gp, send_gc, recv_gc,
    send_gg, recv_gg,
):
    wide = lax.axis_index("wide")
    z = lax.axis_index("narrow")
    core = wide % N_CORE
    x = (wide // N_CORE) % N_X
    y = wide // (N_CORE * N_X)
    q = wide // N_CORE
    z_peers = [device(y, x, core, z + d) for d in range(1, N_Z)]
    z_index = [(z + d) % N_Z for d in range(1, N_Z)]
    xy_offsets = [(a, b) for a in range(N_Y) for b in range(N_X) if a or b]
    xy_peers = [device(y + a, x + b, core, z) for a, b in xy_offsets]
    xy_index = [((y + a) % N_Y) * N_X + (x + b) % N_X for a, b in xy_offsets]
    sibling = device(y, x, core + 1, z)
    peers = z_peers + xy_peers + [sibling]

    def band(c):
        return pl.ds(pl.multiple_of(c * GROUP, GROUP), GROUP)

    def load(c):
        return pltpu.make_async_copy(panel_ref.at[band(c)], panel.at[c], in_sem.at[c])

    barrier = pltpu.get_barrier_semaphore()

    def greet(some):
        for peer in some:
            pl.semaphore_signal(barrier, inc=1, device_id=peer, device_id_type=MESH)

    load_signs = pltpu.make_async_copy(signs_hbm, signs_ref, signs_sem)
    load_samples = pltpu.make_async_copy(samples_hbm, samples_ref, samples_sem)
    greet(z_peers)
    load_signs.start()
    load(0).start()
    greet(xy_peers + [sibling])
    for c in range(1, CHUNKS):
        load(c).start()
    load_samples.start()

    def send(over_z, src, target, c, send_sem, recv_sem):
        size = Z_LEN if over_z else P_LEN
        peers, index = (z_peers, z_index) if over_z else (xy_peers, xy_index)
        for peer, place in zip(peers, index):
            pltpu.make_async_remote_copy(
                src_ref=src.at[c, :, lanes(place * size, size)],
                dst_ref=target(lanes((z if over_z else q) * size, size)),
                send_sem=send_sem.at[c],
                recv_sem=recv_sem.at[c],
                device_id=peer,
                device_id_type=MESH,
            ).start()

    def await_bytes(over_z, ref, c, sem):
        part = ref.at[c, :, pl.ds(0, COUNT - (Z_LEN if over_z else P_LEN))]
        pltpu.make_async_copy(part, part, sem.at[c]).wait()

    def mix(c):
        load(c).wait()

        def part(i, carry):
            places = [lanes(p * Z_LEN + i * 512, 512) for p in range(N_Z)]
            values = [panel[c, :, place] * signs_ref[:, place].astype(F32) for place in places]
            for place, value in zip(places, butterflies(values)):
                s0[c, :, place] = value
            return carry

        lax.fori_loop(0, Z_LEN // 512, part, 0)

    def send_z(c):
        send(True, s0, lambda place: r1.at[c, :, place], c, send1, recv1)

    load_signs.wait()
    mix(0)
    pl.semaphore_wait(barrier, len(peers))
    send_z(0)

    def begin(c, carry):
        mix(c)
        send_z(c)
        return carry

    lax.fori_loop(1, CHUNKS, begin, 0)

    load_samples.wait()
    weight[...] = jnp.zeros_like(weight)

    def mark(i, carry):
        rows = samples_ref[pl.ds(pl.multiple_of(i * 8, 8), 8), :]
        offsets = rows - wide * (N_Z * COUNT)
        place = jnp.bitwise_and(jnp.right_shift(offsets, 11), N_Z - 1)
        inside = (jnp.right_shift(offsets, 17) == 0) & (place == z)
        inner = jnp.bitwise_and(jnp.right_shift(offsets, 7), Z_LEN // 128 - 1)
        high = jnp.where(inside, jnp.right_shift(offsets, 14) * (Z_LEN // 128) + inner, -1)
        low = jnp.bitwise_and(offsets, 127)
        places = lax.broadcasted_iota(jnp.int32, (128, 128), 0)
        total = jnp.zeros((128, 128), F32)
        for r in range(0, 8, 2):
            above = [jnp.where(places == high[k:k + 1], 1.0, 0.0) for k in (r, r + 1)]
            below = [jnp.where(places == low[k:k + 1], 1.0, 0.0) for k in (r, r + 1)]
            total += lax.dot_general(
                jnp.concatenate(above, axis=1).astype(BF16),
                jnp.concatenate(below, axis=1).astype(BF16),
                NT,
                preferred_element_type=F32,
            )
        weight[...] += total
        return carry

    lax.fori_loop(0, 16, mark, 0)

    common = jnp.bitwise_and(
        lax.broadcasted_iota(jnp.int32, (INNER, INNER), 0),
        lax.broadcasted_iota(jnp.int32, (INNER, INNER), 1),
    )
    for shift in (4, 2, 1):
        common = jnp.bitwise_xor(common, jnp.right_shift(common, shift))
    h_ref[...] = jnp.where(jnp.bitwise_and(common, 1) == 0, 1.0 / root, -1.0 / root).astype(BF16)

    def plane_out(c):
        await_bytes(True, r1, c, recv1)
        mine = lanes(z * Z_LEN, Z_LEN)
        r1[c, :, mine] = s0[c, :, mine]

        def inner(i, carry):
            places = [lanes(p * Z_LEN + i * INNER, INNER) for p in range(N_Z)]
            values = butterflies([r1[c, :, place] for place in places])
            rows = []
            for value in values:
                rows += [value, value - value.astype(BF16).astype(F32)]
            stacked = jnp.concatenate(rows, axis=0).astype(BF16)
            done = jnp.dot(stacked, h_ref[...], preferred_element_type=F32)
            for p, place in enumerate(places):
                s1[c, :, place] = done[16 * p:16 * p + 8] + done[16 * p + 8:16 * p + 16]
            return carry

        lax.fori_loop(0, Z_LEN // INNER, inner, 0)

        def outer(p, carry):
            places = [lanes(p * Z_LEN + i * INNER, INNER) for i in range(Z_LEN // INNER)]
            values = butterflies([s1[c, :, place] for place in places])
            for place, value in zip(places, values):
                s1[c, :, place] = value
            return carry

        lax.fori_loop(0, N_Z, outer, 0)
        send(False, s1, lambda place: r2.at[c, :, place], c, send2, recv2)

    def plane_back(c):
        await_bytes(False, r2, c, recv2)
        mine = lanes(q * P_LEN, P_LEN)
        r2[c, :, mine] = s1[c, :, mine]

        def part(i, carry):
            places = [lanes(p * P_LEN + i * 256, 256) for p in range(PLANE)]
            values = butterflies([r2[c, :, place] for place in places])
            for place, value in zip(places, values):
                s2[c, :, place] = value
            return carry

        lax.fori_loop(0, P_LEN // 256, part, 0)
        send(False, s2, lambda place: r3.at[c, :, place], c, send3, recv3)

    def core_copy(c):
        return pltpu.make_async_remote_copy(
            src_ref=r3.at[c], dst_ref=e.at[c], send_sem=send_core.at[c], recv_sem=recv_core.at[c],
            device_id=sibling, device_id_type=MESH,
        )

    def core_out(c):
        await_bytes(False, r3, c, recv3)
        mine = lanes(q * P_LEN, P_LEN)
        r3[c, :, mine] = s2[c, :, mine]
        core_copy(c).start()

    flip = 1.0 - 2.0 * core.astype(F32)

    def keep(c):
        mine = lanes(z * Z_LEN, Z_LEN)
        return pltpu.make_async_copy(s3.at[c, :, mine], mixed_ref.at[band(c), mine], own_sem.at[c])

    def last(c):
        core_copy(c).wait_recv()

        def slab(i, carry):
            place = lanes(i * 1024, 1024)
            values = e[c, :, place] + flip * r3[c, :, place]
            s3[c, :, place] = values
            rows = weight[pl.ds(pl.multiple_of(i * 8, 8), 8), :]
            mask = jnp.concatenate([rows[k:k + 1] for k in range(8)], axis=1)
            values = values * mask
            low = values - values.astype(BF16).astype(F32)
            both = jnp.concatenate([values, low], axis=0).astype(BF16)
            tw[pl.ds(pl.multiple_of(c * 16, 16), 16), place] = both
            return carry

        lax.fori_loop(0, COUNT // 1024, slab, 0)
        keep(c).start()

    def z_back(c, carry):
        send(True, s3, lambda place: mixed_ref.at[band(c), place], c, send4, recv4)
        return carry

    def step(c, carry):
        plane_out(c)
        plane_back(c - 1)
        core_out(c - 2)
        last(c - 2)
        return carry

    def early(c, carry):
        step(c, carry)
        z_back(c - 2, carry)
        return carry

    plane_out(0)
    plane_out(1)
    plane_back(0)
    lax.fori_loop(2, AHEAD + 2, early, 0)
    lax.fori_loop(AHEAD + 2, CHUNKS, step, 0)
    plane_back(CHUNKS - 1)
    core_out(CHUNKS - 2)
    last(CHUNKS - 2)
    core_out(CHUNKS - 1)
    last(CHUNKS - 1)

    def product(i, total):
        part = tw[:, lanes(i * 2048, 2048)]
        return total + lax.dot_general(part, part, NT, preferred_element_type=F32)

    total = lax.fori_loop(0, COUNT // 2048, product, jnp.zeros((128, 128), F32))
    rows = jnp.concatenate(
        [total[16 * c:16 * c + 8] + total[16 * c + 8:16 * c + 16] for c in range(CHUNKS)], axis=0
    )
    lane = lax.broadcasted_iota(jnp.int32, (128, 128), 0)
    column = lax.broadcasted_iota(jnp.int32, (128, 128), 1)
    chosen = jnp.where((lane // 16) * 8 + lane % 8 == column, 1.0, 0.0)
    g_own[...] = jnp.dot(rows, chosen, precision=lax.Precision.HIGHEST, preferred_element_type=F32)

    for peer, place in zip(z_peers, z_index):
        pltpu.make_async_remote_copy(
            src_ref=g_own.at[band(place)], dst_ref=g_z.at[z], send_sem=send_gz.at[0],
            recv_sem=recv_gz.at[0], device_id=peer, device_id_type=MESH,
        ).start()
    z_back(AHEAD, 0)
    g_z[z] = g_own[band(z)]
    others = g_z.at[pl.ds(0, N_Z - 1)]
    pltpu.make_async_copy(others, others, recv_gz.at[0]).wait()
    g_zsum[...] = functools.reduce(lambda a, b: a + b, [g_z[k] for k in range(N_Z)])
    for peer in xy_peers:
        pltpu.make_async_remote_copy(
            src_ref=g_zsum, dst_ref=g_plane.at[q], send_sem=send_gp.at[0],
            recv_sem=recv_gp.at[0], device_id=peer, device_id_type=MESH,
        ).start()
    g_plane[q] = g_zsum[...]
    planes = g_plane.at[pl.ds(0, PLANE - 1)]
    pltpu.make_async_copy(planes, planes, recv_gp.at[0]).wait()
    g_psum[...] = functools.reduce(lambda a, b: a + b, [g_plane[k] for k in range(PLANE)])
    to_sibling = pltpu.make_async_remote_copy(
        src_ref=g_psum, dst_ref=g_core, send_sem=send_gc.at[0],
        recv_sem=recv_gc.at[0], device_id=sibling, device_id_type=MESH,
    )
    to_sibling.start()
    to_sibling.wait()
    gram[band(z)] = g_psum[...] + g_core[...]
    for peer in z_peers:
        pltpu.make_async_remote_copy(
            src_ref=gram.at[band(z)], dst_ref=gram.at[band(z)], send_sem=send_gg.at[0],
            recv_sem=recv_gg.at[0], device_id=peer, device_id_type=MESH,
        ).start()
    lax.fori_loop(AHEAD + 1, CHUNKS, z_back, 0)
    bands = gram.at[pl.ds(0, COLS - GROUP)]
    pltpu.make_async_copy(bands, bands, recv_gg.at[0]).wait()

    row = lax.broadcasted_iota(jnp.int32, (COLS, 2 * COLS), 0)
    column = lax.broadcasted_iota(jnp.int32, (COLS, 2 * COLS), 1)
    start = jnp.where(
        column < COLS, gram[...] * scale, jnp.where(column - COLS == row, 1.0, 0.0)
    )

    def eliminate(k, values):
        line = jnp.sum(jnp.where(row == k, values, 0.0), axis=0, keepdims=True)
        factor = jnp.sum(jnp.where((column == k) & (row > k), values, 0.0), axis=1, keepdims=True)
        pivot = jnp.sum(jnp.where(column[:1] == k, line, 0.0), axis=1, keepdims=True)
        return values - factor * (line / pivot)

    done = lax.fori_loop(0, COLS, eliminate, start)
    diagonal = jnp.sum(jnp.where(row == column, done, 0.0), axis=1, keepdims=True)
    done = done / jnp.sqrt(diagonal)
    square = done[:, :COLS]
    r_ref[...] = jnp.where(row[:, :COLS] <= column[:, :COLS], square * (1.0 / root), 0.0)
    inverse = done[:, COLS:] * root
    high = inverse.astype(BF16)
    low = (inverse - high.astype(F32)).astype(BF16)
    left = jnp.concatenate([high, low, high], axis=1)

    def multiply(i, carry):
        place = lanes(i * 1024, 1024)
        values = jnp.concatenate([panel[c, :, place] for c in range(CHUNKS)], axis=0)
        values_high = values.astype(BF16)
        values_low = (values - values_high.astype(F32)).astype(BF16)
        right = jnp.concatenate([values_high, values_high, values_low], axis=0)
        out[:, place] = jnp.dot(left, right, preferred_element_type=F32)
        return carry

    lax.fori_loop(0, COUNT // 1024, multiply, 0)

    pltpu.make_async_copy(others, others, send_gz.at[0]).wait()
    pltpu.make_async_copy(planes, planes, send_gp.at[0]).wait()
    pltpu.make_async_copy(bands, bands, send_gg.at[0]).wait()

    def left_all(c, carry):
        await_bytes(True, s0, c, send1)
        await_bytes(False, s1, c, send2)
        await_bytes(False, s2, c, send3)
        core_copy(c).wait_send()
        keep(c).wait()
        return carry

    lax.fori_loop(0, CHUNKS, left_all, 0)

    def arrived(c, carry):
        await_bytes(True, s3, c, send4)
        part = mixed_ref.at[band(c), pl.ds(0, COUNT - Z_LEN)]
        pltpu.make_async_copy(part, part, recv4.at[c]).wait()
        return carry

    lax.fori_loop(0, CHUNKS, arrived, 0)


def move_kernel(mixed_in, r_in, precond_in, mixed_ref, r_ref, precond_ref, sem):
    pairs = [(mixed_in, mixed_ref), (precond_in, precond_ref), (r_in, r_ref)]
    copies = [pltpu.make_async_copy(a, b, sem.at[i]) for i, (a, b) in enumerate(pairs)]
    for copy in copies:
        copy.start()
    for copy in copies:
        copy.wait()


def body(panel, signs, sample_rows):
    cols, count = panel.shape
    total = count * lax.axis_size("wide") * lax.axis_size("narrow")
    root = math.sqrt(total)
    any_space = pl.BlockSpec(memory_space=pl.ANY)
    vmem = pl.BlockSpec(memory_space=pltpu.VMEM)
    chunked = pltpu.VMEM((CHUNKS, GROUP, count), F32)
    small = pltpu.VMEM((GROUP, 128), F32)
    dma = pltpu.SemaphoreType.DMA
    shapes = [(cols, count), (cols, cols), (cols, count)]
    arguments = (panel, signs.reshape(1, count), sample_rows.reshape(-1, 128))
    results = pl.pallas_call(
        functools.partial(mix_kernel, total / sample_rows.shape[0], root),
        out_shape=tuple(pltpu.VMEM(shape, F32) for shape in shapes),
        in_specs=[any_space] * 3,
        out_specs=(vmem,) * 3,
        scratch_shapes=[
            chunked,
            pltpu.VMEM((1, count), jnp.int32),
            pltpu.VMEM((128, 128), jnp.int32),
            pltpu.VMEM((INNER, INNER), BF16),
        ]
        + [chunked] * 8
        + [
            pltpu.VMEM((2 * cols, count), BF16),
            pltpu.VMEM((128, 128), F32),
            pltpu.VMEM((cols, 128), F32),
            pltpu.VMEM((N_Z, GROUP, 128), F32),
            small,
            pltpu.VMEM((PLANE, GROUP, 128), F32),
            small,
            small,
            pltpu.VMEM((cols, 128), F32),
        ]
        + [dma((CHUNKS,))] * 2
        + [dma, dma]
        + [dma((CHUNKS,))] * 10
        + [dma((1,))] * 8,
        compiler_params=pltpu.CompilerParams(
            collective_id=0, has_side_effects=True, vmem_limit_bytes=44 * 1024 * 1024
        ),
    )(*(pltpu.with_memory_space_constraint(one, pltpu.HBM) for one in arguments))
    return pl.pallas_call(
        move_kernel,
        out_shape=tuple(jax.ShapeDtypeStruct(shape, F32) for shape in shapes),
        in_specs=[any_space] * 3,
        out_specs=(any_space,) * 3,
        scratch_shapes=[dma((3,))],
        compiler_params=pltpu.CompilerParams(vmem_limit_bytes=1024 * 1024),
    )(*results)


def solution(mesh):
    in_specs = (P(None, ("wide", "narrow")), P(("wide", "narrow")), P())
    out_specs = (P(None, ("wide", "narrow")), P(), P(None, ("wide", "narrow")))
    return jax.shard_map(body, mesh=mesh, in_specs=in_specs, out_specs=out_specs, check_vma=False)
```

```python
import functools
import math

import jax
import jax.numpy as jnp
from jax import lax
from jax.experimental import pallas as pl
from jax.experimental.pallas import tpu as pltpu
from jax.sharding import PartitionSpec as P

MESH = pl.DeviceIdType.MESH
F32 = jnp.float32
BF16 = jnp.bfloat16
NT = (((1,), (1,)), ((), ()))

N_Y, N_X, N_CORE, N_Z = 4, 4, 2, 8
PLANE = N_Y * N_X
COLS = 64
COUNT = 16384
GROUP = 8
CHUNKS = COLS // GROUP
DESK, TELLER = 6, 5
AHEAD = 3
Z_LEN = COUNT // N_Z
P_LEN = COUNT // PLANE
INNER = 256


def butterflies(parts):
    parts = list(parts)
    half = 1
    while half < len(parts):
        for low in range(len(parts)):
            if not low & half:
                first, second = parts[low], parts[low | half]
                parts[low], parts[low | half] = first + second, first - second
        half *= 2
    return parts


def lanes(start, size):
    return pl.ds(pl.multiple_of(start, 128), size)


def device(y, x, core, z):
    return (((y % N_Y) * N_X + x % N_X) * N_CORE + core % N_CORE, z % N_Z)


def mix_kernel(
    scale, root, panel_ref, signs_hbm, samples_hbm, mixed_ref, r_ref, out,
    panel, signs_ref, samples_ref, h_ref, s0, r1, s1, r2, s2, r3, e, s3, tw, weight,
    g_own, g_z, g_zsum, g_plane, g_psum, g_core, gram,
    in_sem, own_sem, signs_sem, samples_sem, send1, recv1, send2, recv2, send3, recv3, send4, recv4,
    send_core, recv_core, send_gz, recv_gz, send_gp, recv_gp, send_gc, recv_gc,
    send_gg, recv_gg, ring_sem, plane_sem,
):
    wide = lax.axis_index("wide")
    z = lax.axis_index("narrow")
    core = wide % N_CORE
    x = (wide // N_CORE) % N_X
    y = wide // (N_CORE * N_X)
    q = wide // N_CORE
    z_peers = [device(y, x, core, z + d) for d in range(1, N_Z)]
    z_index = [(z + d) % N_Z for d in range(1, N_Z)]
    xy_offsets = [(a, b) for a in range(N_Y) for b in range(N_X) if a or b]
    xy_peers = [device(y + a, x + b, core, z) for a, b in xy_offsets]
    xy_index = [((y + a) % N_Y) * N_X + (x + b) % N_X for a, b in xy_offsets]
    sibling = device(y, x, core + 1, z)

    def band(c):
        return pl.ds(pl.multiple_of(c * GROUP, GROUP), GROUP)

    def load(c):
        return pltpu.make_async_copy(panel_ref.at[band(c)], panel.at[c], in_sem.at[c])

    barrier = pltpu.get_barrier_semaphore()

    def greet(some):
        for peer in some:
            pl.semaphore_signal(barrier, inc=1, device_id=peer, device_id_type=MESH)

    load_signs = pltpu.make_async_copy(signs_hbm, signs_ref, signs_sem)
    load_samples = pltpu.make_async_copy(samples_hbm, samples_ref, samples_sem)
    for d in range(1, N_Z):
        pl.when((z + d) % N_Z != DESK)(functools.partial(greet, [z_peers[d - 1]]))
    load_signs.start()
    load(0).start()

    @pl.when(z == TELLER)
    def _():
        pl.semaphore_wait(barrier, N_Z - 1)
        pl.semaphore_signal(
            ring_sem, inc=1, device_id=device(y, x, core, DESK), device_id_type=MESH
        )

    for c in range(1, CHUNKS):
        load(c).start()
    load_samples.start()

    def send(over_z, src, target, c, send_sem, recv_sem):
        size = Z_LEN if over_z else P_LEN
        peers, index = (z_peers, z_index) if over_z else (xy_peers, xy_index)
        for peer, place in zip(peers, index):
            pltpu.make_async_remote_copy(
                src_ref=src.at[c, :, lanes(place * size, size)],
                dst_ref=target(lanes((z if over_z else q) * size, size)),
                send_sem=send_sem.at[c],
                recv_sem=recv_sem.at[c],
                device_id=peer,
                device_id_type=MESH,
            ).start()

    def await_bytes(over_z, ref, c, sem):
        part = ref.at[c, :, pl.ds(0, COUNT - (Z_LEN if over_z else P_LEN))]
        pltpu.make_async_copy(part, part, sem.at[c]).wait()

    def mix(c):
        load(c).wait()

        def part(i, carry):
            places = [lanes(p * Z_LEN + i * 512, 512) for p in range(N_Z)]
            values = [panel[c, :, place] * signs_ref[:, place].astype(F32) for place in places]
            for place, value in zip(places, butterflies(values)):
                s0[c, :, place] = value
            return carry

        lax.fori_loop(0, Z_LEN // 512, part, 0)

    def send_z(c):
        send(True, s0, lambda place: r1.at[c, :, place], c, send1, recv1)

    load_signs.wait()
    mix(0)

    @pl.when((z != TELLER) & (z != DESK))
    def _():
        pl.semaphore_wait(barrier, N_Z - 1)

    @pl.when(z == DESK)
    def _():
        pl.semaphore_wait(ring_sem, 1)

    send_z(0)

    @pl.when(z == DESK)
    def _():
        greet(xy_peers + [sibling])


    def begin(c, carry):
        mix(c)
        send_z(c)
        return carry

    lax.fori_loop(1, CHUNKS, begin, 0)

    load_samples.wait()
    weight[...] = jnp.zeros_like(weight)

    def mark(i, carry):
        rows = samples_ref[pl.ds(pl.multiple_of(i * 8, 8), 8), :]
        offsets = rows - wide * (N_Z * COUNT)
        place = jnp.bitwise_and(jnp.right_shift(offsets, 11), N_Z - 1)
        inside = (jnp.right_shift(offsets, 17) == 0) & (place == z)
        inner = jnp.bitwise_and(jnp.right_shift(offsets, 7), Z_LEN // 128 - 1)
        high = jnp.where(inside, jnp.right_shift(offsets, 14) * (Z_LEN // 128) + inner, -1)
        low = jnp.bitwise_and(offsets, 127)
        places = lax.broadcasted_iota(jnp.int32, (128, 128), 0)
        total = jnp.zeros((128, 128), F32)
        for r in range(0, 8, 2):
            above = [jnp.where(places == high[k:k + 1], 1.0, 0.0) for k in (r, r + 1)]
            below = [jnp.where(places == low[k:k + 1], 1.0, 0.0) for k in (r, r + 1)]
            total += lax.dot_general(
                jnp.concatenate(above, axis=1).astype(BF16),
                jnp.concatenate(below, axis=1).astype(BF16),
                NT,
                preferred_element_type=F32,
            )
        weight[...] += total
        return carry

    lax.fori_loop(0, 16, mark, 0)

    @pl.when(z == DESK)
    def _():
        pl.semaphore_wait(barrier, PLANE)
        for peer in z_peers:
            pl.semaphore_signal(plane_sem, inc=1, device_id=peer, device_id_type=MESH)

    @pl.when(z != DESK)
    def _():
        pl.semaphore_wait(plane_sem, 1)

    common = jnp.bitwise_and(
        lax.broadcasted_iota(jnp.int32, (INNER, INNER), 0),
        lax.broadcasted_iota(jnp.int32, (INNER, INNER), 1),
    )
    for shift in (4, 2, 1):
        common = jnp.bitwise_xor(common, jnp.right_shift(common, shift))
    h_ref[...] = jnp.where(jnp.bitwise_and(common, 1) == 0, 1.0 / root, -1.0 / root).astype(BF16)

    def plane_out(c):
        await_bytes(True, r1, c, recv1)
        mine = lanes(z * Z_LEN, Z_LEN)
        r1[c, :, mine] = s0[c, :, mine]

        def inner(i, carry):
            places = [lanes(p * Z_LEN + i * INNER, INNER) for p in range(N_Z)]
            values = butterflies([r1[c, :, place] for place in places])
            rows = []
            for value in values:
                rows += [value, value - value.astype(BF16).astype(F32)]
            stacked = jnp.concatenate(rows, axis=0).astype(BF16)
            done = jnp.dot(stacked, h_ref[...], preferred_element_type=F32)
            for p, place in enumerate(places):
                s1[c, :, place] = done[16 * p:16 * p + 8] + done[16 * p + 8:16 * p + 16]
            return carry

        lax.fori_loop(0, Z_LEN // INNER, inner, 0)

        def outer(p, carry):
            places = [lanes(p * Z_LEN + i * INNER, INNER) for i in range(Z_LEN // INNER)]
            values = butterflies([s1[c, :, place] for place in places])
            for place, value in zip(places, values):
                s1[c, :, place] = value
            return carry

        lax.fori_loop(0, N_Z, outer, 0)
        send(False, s1, lambda place: r2.at[c, :, place], c, send2, recv2)

    def plane_back(c):
        await_bytes(False, r2, c, recv2)
        mine = lanes(q * P_LEN, P_LEN)
        r2[c, :, mine] = s1[c, :, mine]

        def part(i, carry):
            places = [lanes(p * P_LEN + i * 256, 256) for p in range(PLANE)]
            values = butterflies([r2[c, :, place] for place in places])
            for place, value in zip(places, values):
                s2[c, :, place] = value
            return carry

        lax.fori_loop(0, P_LEN // 256, part, 0)
        send(False, s2, lambda place: r3.at[c, :, place], c, send3, recv3)

    def core_copy(c):
        return pltpu.make_async_remote_copy(
            src_ref=r3.at[c], dst_ref=e.at[c], send_sem=send_core.at[c], recv_sem=recv_core.at[c],
            device_id=sibling, device_id_type=MESH,
        )

    def core_out(c):
        await_bytes(False, r3, c, recv3)
        mine = lanes(q * P_LEN, P_LEN)
        r3[c, :, mine] = s2[c, :, mine]
        core_copy(c).start()

    flip = 1.0 - 2.0 * core.astype(F32)

    def keep(c):
        mine = lanes(z * Z_LEN, Z_LEN)
        return pltpu.make_async_copy(s3.at[c, :, mine], mixed_ref.at[band(c), mine], own_sem.at[c])

    def last(c):
        core_copy(c).wait_recv()

        def slab(i, carry):
            place = lanes(i * 1024, 1024)
            values = e[c, :, place] + flip * r3[c, :, place]
            s3[c, :, place] = values
            rows = weight[pl.ds(pl.multiple_of(i * 8, 8), 8), :]
            mask = jnp.concatenate([rows[k:k + 1] for k in range(8)], axis=1)
            values = values * mask
            low = values - values.astype(BF16).astype(F32)
            both = jnp.concatenate([values, low], axis=0).astype(BF16)
            tw[pl.ds(pl.multiple_of(c * 16, 16), 16), place] = both
            return carry

        lax.fori_loop(0, COUNT // 1024, slab, 0)
        keep(c).start()

    def z_back(c, carry):
        send(True, s3, lambda place: mixed_ref.at[band(c), place], c, send4, recv4)
        return carry

    def step(c, carry):
        plane_out(c)
        plane_back(c - 1)
        core_out(c - 2)
        last(c - 2)
        return carry

    def early(c, carry):
        step(c, carry)
        z_back(c - 2, carry)
        return carry

    plane_out(0)
    plane_out(1)
    plane_back(0)
    lax.fori_loop(2, AHEAD + 2, early, 0)
    lax.fori_loop(AHEAD + 2, CHUNKS, step, 0)
    plane_back(CHUNKS - 1)
    core_out(CHUNKS - 2)
    last(CHUNKS - 2)
    core_out(CHUNKS - 1)
    last(CHUNKS - 1)

    def product(i, total):
        part = tw[:, lanes(i * 2048, 2048)]
        return total + lax.dot_general(part, part, NT, preferred_element_type=F32)

    total = lax.fori_loop(0, COUNT // 2048, product, jnp.zeros((128, 128), F32))
    rows = jnp.concatenate(
        [total[16 * c:16 * c + 8] + total[16 * c + 8:16 * c + 16] for c in range(CHUNKS)], axis=0
    )
    lane = lax.broadcasted_iota(jnp.int32, (128, 128), 0)
    column = lax.broadcasted_iota(jnp.int32, (128, 128), 1)
    chosen = jnp.where((lane // 16) * 8 + lane % 8 == column, 1.0, 0.0)
    g_own[...] = jnp.dot(rows, chosen, precision=lax.Precision.HIGHEST, preferred_element_type=F32)

    for peer, place in zip(z_peers, z_index):
        pltpu.make_async_remote_copy(
            src_ref=g_own.at[band(place)], dst_ref=g_z.at[z], send_sem=send_gz.at[0],
            recv_sem=recv_gz.at[0], device_id=peer, device_id_type=MESH,
        ).start()
    z_back(AHEAD, 0)
    z_back(AHEAD + 1, 0)
    g_z[z] = g_own[band(z)]
    others = g_z.at[pl.ds(0, N_Z - 1)]
    pltpu.make_async_copy(others, others, recv_gz.at[0]).wait()
    g_zsum[...] = functools.reduce(lambda a, b: a + b, [g_z[k] for k in range(N_Z)])
    for peer in xy_peers:
        pltpu.make_async_remote_copy(
            src_ref=g_zsum, dst_ref=g_plane.at[q], send_sem=send_gp.at[0],
            recv_sem=recv_gp.at[0], device_id=peer, device_id_type=MESH,
        ).start()
    g_plane[q] = g_zsum[...]
    planes = g_plane.at[pl.ds(0, PLANE - 1)]
    pltpu.make_async_copy(planes, planes, recv_gp.at[0]).wait()
    g_psum[...] = functools.reduce(lambda a, b: a + b, [g_plane[k] for k in range(PLANE)])
    to_sibling = pltpu.make_async_remote_copy(
        src_ref=g_psum, dst_ref=g_core, send_sem=send_gc.at[0],
        recv_sem=recv_gc.at[0], device_id=sibling, device_id_type=MESH,
    )
    to_sibling.start()
    to_sibling.wait()
    gram[band(z)] = g_psum[...] + g_core[...]
    for peer in z_peers:
        pltpu.make_async_remote_copy(
            src_ref=gram.at[band(z)], dst_ref=gram.at[band(z)], send_sem=send_gg.at[0],
            recv_sem=recv_gg.at[0], device_id=peer, device_id_type=MESH,
        ).start()
    lax.fori_loop(AHEAD + 2, CHUNKS, z_back, 0)
    bands = gram.at[pl.ds(0, COLS - GROUP)]
    pltpu.make_async_copy(bands, bands, recv_gg.at[0]).wait()

    row = lax.broadcasted_iota(jnp.int32, (COLS, 2 * COLS), 0)
    column = lax.broadcasted_iota(jnp.int32, (COLS, 2 * COLS), 1)
    start = jnp.where(
        column < COLS, gram[...] * scale, jnp.where(column - COLS == row, 1.0, 0.0)
    )

    def eliminate(k, values):
        line = jnp.sum(jnp.where(row == k, values, 0.0), axis=0, keepdims=True)
        factor = jnp.sum(jnp.where((column == k) & (row > k), values, 0.0), axis=1, keepdims=True)
        pivot = jnp.sum(jnp.where(column[:1] == k, line, 0.0), axis=1, keepdims=True)
        return values - factor * (line / pivot)

    done = lax.fori_loop(0, COLS, eliminate, start)
    diagonal = jnp.sum(jnp.where(row == column, done, 0.0), axis=1, keepdims=True)
    done = done / jnp.sqrt(diagonal)
    square = done[:, :COLS]
    r_ref[...] = jnp.where(row[:, :COLS] <= column[:, :COLS], square * (1.0 / root), 0.0)
    inverse = done[:, COLS:] * root
    high = inverse.astype(BF16)
    low = (inverse - high.astype(F32)).astype(BF16)
    left = jnp.concatenate([high, low, high], axis=1)

    def multiply(i, carry):
        place = lanes(i * 1024, 1024)
        values = jnp.concatenate([panel[c, :, place] for c in range(CHUNKS)], axis=0)
        values_high = values.astype(BF16)
        values_low = (values - values_high.astype(F32)).astype(BF16)
        right = jnp.concatenate([values_high, values_high, values_low], axis=0)
        out[:, place] = jnp.dot(left, right, preferred_element_type=F32)
        return carry

    lax.fori_loop(0, COUNT // 1024, multiply, 0)

    pltpu.make_async_copy(others, others, send_gz.at[0]).wait()
    pltpu.make_async_copy(planes, planes, send_gp.at[0]).wait()
    pltpu.make_async_copy(bands, bands, send_gg.at[0]).wait()

    def left_all(c, carry):
        await_bytes(True, s0, c, send1)
        await_bytes(False, s1, c, send2)
        await_bytes(False, s2, c, send3)
        core_copy(c).wait_send()
        keep(c).wait()
        return carry

    lax.fori_loop(0, CHUNKS, left_all, 0)

    def arrived(c, carry):
        await_bytes(True, s3, c, send4)
        part = mixed_ref.at[band(c), pl.ds(0, COUNT - Z_LEN)]
        pltpu.make_async_copy(part, part, recv4.at[c]).wait()
        return carry

    lax.fori_loop(0, CHUNKS, arrived, 0)


def move_kernel(mixed_in, r_in, precond_in, mixed_ref, r_ref, precond_ref, sem):
    pairs = [(mixed_in, mixed_ref), (precond_in, precond_ref), (r_in, r_ref)]
    copies = [pltpu.make_async_copy(a, b, sem.at[i]) for i, (a, b) in enumerate(pairs)]
    for copy in copies:
        copy.start()
    for copy in copies:
        copy.wait()


def body(panel, signs, sample_rows):
    cols, count = panel.shape
    total = count * lax.axis_size("wide") * lax.axis_size("narrow")
    root = math.sqrt(total)
    any_space = pl.BlockSpec(memory_space=pl.ANY)
    vmem = pl.BlockSpec(memory_space=pltpu.VMEM)
    chunked = pltpu.VMEM((CHUNKS, GROUP, count), F32)
    small = pltpu.VMEM((GROUP, 128), F32)
    dma = pltpu.SemaphoreType.DMA
    shapes = [(cols, count), (cols, cols), (cols, count)]
    arguments = (panel, signs.reshape(1, count), sample_rows.reshape(-1, 128))
    results = pl.pallas_call(
        functools.partial(mix_kernel, total / sample_rows.shape[0], root),
        out_shape=tuple(pltpu.VMEM(shape, F32) for shape in shapes),
        in_specs=[any_space] * 3,
        out_specs=(vmem,) * 3,
        scratch_shapes=[
            chunked,
            pltpu.VMEM((1, count), jnp.int32),
            pltpu.VMEM((128, 128), jnp.int32),
            pltpu.VMEM((INNER, INNER), BF16),
        ]
        + [chunked] * 8
        + [
            pltpu.VMEM((2 * cols, count), BF16),
            pltpu.VMEM((128, 128), F32),
            pltpu.VMEM((cols, 128), F32),
            pltpu.VMEM((N_Z, GROUP, 128), F32),
            small,
            pltpu.VMEM((PLANE, GROUP, 128), F32),
            small,
            small,
            pltpu.VMEM((cols, 128), F32),
        ]
        + [dma((CHUNKS,))] * 2
        + [dma, dma]
        + [dma((CHUNKS,))] * 10
        + [dma((1,))] * 8
        + [pltpu.SemaphoreType.REGULAR] * 2,
        compiler_params=pltpu.CompilerParams(
            collective_id=0, has_side_effects=True, vmem_limit_bytes=44 * 1024 * 1024
        ),
    )(*(pltpu.with_memory_space_constraint(one, pltpu.HBM) for one in arguments))
    return pl.pallas_call(
        move_kernel,
        out_shape=tuple(jax.ShapeDtypeStruct(shape, F32) for shape in shapes),
        in_specs=[any_space] * 3,
        out_specs=(any_space,) * 3,
        scratch_shapes=[dma((3,))],
        compiler_params=pltpu.CompilerParams(vmem_limit_bytes=1024 * 1024),
    )(*results)


def solution(mesh):
    in_specs = (P(None, ("wide", "narrow")), P(("wide", "narrow")), P())
    out_specs = (P(None, ("wide", "narrow")), P(), P(None, ("wide", "narrow")))
    return jax.shard_map(body, mesh=mesh, in_specs=in_specs, out_specs=out_specs, check_vma=False)
```

```python
import functools
import math

import jax
import jax.numpy as jnp
from jax import lax
from jax.experimental import pallas as pl
from jax.experimental.pallas import tpu as pltpu
from jax.sharding import PartitionSpec as P

MESH = pl.DeviceIdType.MESH
F32 = jnp.float32
BF16 = jnp.bfloat16
NT = (((1,), (1,)), ((), ()))

N_Y, N_X, N_CORE, N_Z = 4, 4, 2, 8
PLANE = N_Y * N_X
COLS = 64
COUNT = 16384
GROUP = 8
CHUNKS = COLS // GROUP
DESK, TELLER = 6, 5
AHEAD = 4
Z_LEN = COUNT // N_Z
P_LEN = COUNT // PLANE
INNER = 256


def butterflies(parts):
    parts = list(parts)
    half = 1
    while half < len(parts):
        for low in range(len(parts)):
            if not low & half:
                first, second = parts[low], parts[low | half]
                parts[low], parts[low | half] = first + second, first - second
        half *= 2
    return parts


def pieces(values):
    high = values.astype(BF16).astype(F32)
    rest = values - high
    middle = rest.astype(BF16).astype(F32)
    return [high, middle, rest - middle]


def lanes(start, size):
    return pl.ds(pl.multiple_of(start, 128), size)


def device(y, x, core, z):
    return (((y % N_Y) * N_X + x % N_X) * N_CORE + core % N_CORE, z % N_Z)


def mix_kernel(
    scale, root, panel_ref, signs_hbm, samples_hbm, mixed_ref, r_ref, out,
    panel, signs_ref, samples_ref, h_ref, s0, r1, s1, r2, s2, r3, e, s3, tw, weight,
    g_own, g_z, g_zsum, g_plane, g_psum, g_core, gram,
    in_sem, own_sem, signs_sem, samples_sem, send1, recv1, send2, recv2, send3, recv3, send4, recv4,
    send_core, recv_core, send_gz, recv_gz, send_gp, recv_gp, send_gc, recv_gc,
    send_gg, recv_gg, ring_sem, plane_sem,
):
    wide = lax.axis_index("wide")
    z = lax.axis_index("narrow")
    core = wide % N_CORE
    x = (wide // N_CORE) % N_X
    y = wide // (N_CORE * N_X)
    q = wide // N_CORE
    z_peers = [device(y, x, core, z + d) for d in range(1, N_Z)]
    z_index = [(z + d) % N_Z for d in range(1, N_Z)]
    xy_offsets = [(a, b) for a in range(N_Y) for b in range(N_X) if a or b]
    xy_peers = [device(y + a, x + b, core, z) for a, b in xy_offsets]
    xy_index = [((y + a) % N_Y) * N_X + (x + b) % N_X for a, b in xy_offsets]
    sibling = device(y, x, core + 1, z)

    def band(c):
        return pl.ds(pl.multiple_of(c * GROUP, GROUP), GROUP)

    def load(c):
        return pltpu.make_async_copy(panel_ref.at[band(c)], panel.at[c], in_sem.at[c])

    barrier = pltpu.get_barrier_semaphore()

    def greet(some):
        for peer in some:
            pl.semaphore_signal(barrier, inc=1, device_id=peer, device_id_type=MESH)

    load_signs = pltpu.make_async_copy(signs_hbm, signs_ref, signs_sem)
    load_samples = pltpu.make_async_copy(samples_hbm, samples_ref, samples_sem)
    for d in range(1, N_Z):
        pl.when((z + d) % N_Z != DESK)(functools.partial(greet, [z_peers[d - 1]]))
    load_signs.start()
    load(0).start()

    @pl.when(z == TELLER)
    def _():
        pl.semaphore_wait(barrier, N_Z - 1)
        pl.semaphore_signal(
            ring_sem, inc=1, device_id=device(y, x, core, DESK), device_id_type=MESH
        )

    for c in range(1, CHUNKS):
        load(c).start()
    load_samples.start()

    def send(over_z, src, target, c, send_sem, recv_sem):
        size = Z_LEN if over_z else P_LEN
        peers, index = (z_peers, z_index) if over_z else (xy_peers, xy_index)
        for peer, place in zip(peers, index):
            pltpu.make_async_remote_copy(
                src_ref=src.at[c, :, lanes(place * size, size)],
                dst_ref=target(lanes((z if over_z else q) * size, size)),
                send_sem=send_sem.at[c],
                recv_sem=recv_sem.at[c],
                device_id=peer,
                device_id_type=MESH,
            ).start()

    def await_bytes(over_z, ref, c, sem):
        part = ref.at[c, :, pl.ds(0, COUNT - (Z_LEN if over_z else P_LEN))]
        pltpu.make_async_copy(part, part, sem.at[c]).wait()

    def mix(c):
        load(c).wait()

        def part(i, carry):
            places = [lanes(p * Z_LEN + i * 512, 512) for p in range(N_Z)]
            values = [panel[c, :, place] * signs_ref[:, place].astype(F32) for place in places]
            for place, value in zip(places, butterflies(values)):
                s0[c, :, place] = value
            return carry

        lax.fori_loop(0, Z_LEN // 512, part, 0)

    def send_z(c):
        send(True, s0, lambda place: r1.at[c, :, place], c, send1, recv1)

    load_signs.wait()
    mix(0)

    @pl.when((z != TELLER) & (z != DESK))
    def _():
        pl.semaphore_wait(barrier, N_Z - 1)

    @pl.when(z == DESK)
    def _():
        pl.semaphore_wait(ring_sem, 1)

    send_z(0)

    @pl.when(z == DESK)
    def _():
        greet(xy_peers + [sibling])


    def begin(c, carry):
        mix(c)
        send_z(c)
        return carry

    lax.fori_loop(1, CHUNKS, begin, 0)

    load_samples.wait()
    weight[...] = jnp.zeros_like(weight)

    def mark(i, carry):
        rows = samples_ref[pl.ds(pl.multiple_of(i * 8, 8), 8), :]
        offsets = rows - wide * (N_Z * COUNT)
        place = jnp.bitwise_and(jnp.right_shift(offsets, 11), N_Z - 1)
        inside = (jnp.right_shift(offsets, 17) == 0) & (place == z)
        inner = jnp.bitwise_and(jnp.right_shift(offsets, 7), Z_LEN // 128 - 1)
        high = jnp.where(inside, jnp.right_shift(offsets, 14) * (Z_LEN // 128) + inner, -1)
        low = jnp.bitwise_and(offsets, 127)
        places = lax.broadcasted_iota(jnp.int32, (128, 128), 0)
        total = jnp.zeros((128, 128), F32)
        for r in range(0, 8, 2):
            above = [jnp.where(places == high[k:k + 1], 1.0, 0.0) for k in (r, r + 1)]
            below = [jnp.where(places == low[k:k + 1], 1.0, 0.0) for k in (r, r + 1)]
            total += lax.dot_general(
                jnp.concatenate(above, axis=1).astype(BF16),
                jnp.concatenate(below, axis=1).astype(BF16),
                NT,
                preferred_element_type=F32,
            )
        weight[...] += total
        return carry

    lax.fori_loop(0, 16, mark, 0)

    @pl.when(z == DESK)
    def _():
        pl.semaphore_wait(barrier, PLANE)
        for peer in z_peers:
            pl.semaphore_signal(plane_sem, inc=1, device_id=peer, device_id_type=MESH)

    @pl.when(z != DESK)
    def _():
        pl.semaphore_wait(plane_sem, 1)

    common = jnp.bitwise_and(
        lax.broadcasted_iota(jnp.int32, (INNER, INNER), 0),
        lax.broadcasted_iota(jnp.int32, (INNER, INNER), 1),
    )
    for shift in (4, 2, 1):
        common = jnp.bitwise_xor(common, jnp.right_shift(common, shift))
    h_ref[...] = jnp.where(jnp.bitwise_and(common, 1) == 0, 1.0 / root, -1.0 / root).astype(BF16)

    def plane_out(c):
        await_bytes(True, r1, c, recv1)
        mine = lanes(z * Z_LEN, Z_LEN)
        r1[c, :, mine] = s0[c, :, mine]

        def inner(i, carry):
            places = [lanes(p * Z_LEN + i * INNER, INNER) for p in range(N_Z)]
            values = butterflies([r1[c, :, place] for place in places])
            rows = []
            for value in values:
                rows += pieces(value)
            stacked = jnp.concatenate(rows, axis=0).astype(BF16)
            done = jnp.dot(stacked, h_ref[...], preferred_element_type=F32)
            for p, place in enumerate(places):
                part = done[24 * p:24 * p + 24]
                s1[c, :, place] = part[:8] + (part[8:16] + part[16:])
            return carry

        lax.fori_loop(0, Z_LEN // INNER, inner, 0)

        def outer(p, carry):
            places = [lanes(p * Z_LEN + i * INNER, INNER) for i in range(Z_LEN // INNER)]
            values = butterflies([s1[c, :, place] for place in places])
            for place, value in zip(places, values):
                s1[c, :, place] = value
            return carry

        lax.fori_loop(0, N_Z, outer, 0)
        send(False, s1, lambda place: r2.at[c, :, place], c, send2, recv2)

    def plane_back(c):
        await_bytes(False, r2, c, recv2)
        mine = lanes(q * P_LEN, P_LEN)
        r2[c, :, mine] = s1[c, :, mine]

        def part(i, carry):
            places = [lanes(p * P_LEN + i * 256, 256) for p in range(PLANE)]
            values = butterflies([r2[c, :, place] for place in places])
            for place, value in zip(places, values):
                s2[c, :, place] = value
            return carry

        lax.fori_loop(0, P_LEN // 256, part, 0)
        send(False, s2, lambda place: r3.at[c, :, place], c, send3, recv3)

    def core_copy(c):
        return pltpu.make_async_remote_copy(
            src_ref=r3.at[c], dst_ref=e.at[c], send_sem=send_core.at[c], recv_sem=recv_core.at[c],
            device_id=sibling, device_id_type=MESH,
        )

    def core_out(c):
        await_bytes(False, r3, c, recv3)
        mine = lanes(q * P_LEN, P_LEN)
        r3[c, :, mine] = s2[c, :, mine]
        core_copy(c).start()

    flip = 1.0 - 2.0 * core.astype(F32)

    def keep(c):
        mine = lanes(z * Z_LEN, Z_LEN)
        return pltpu.make_async_copy(s3.at[c, :, mine], mixed_ref.at[band(c), mine], own_sem.at[c])

    def last(c):
        core_copy(c).wait_recv()

        def slab(i, carry):
            place = lanes(i * 1024, 1024)
            values = e[c, :, place] + flip * r3[c, :, place]
            s3[c, :, place] = values
            rows = weight[pl.ds(pl.multiple_of(i * 8, 8), 8), :]
            mask = jnp.concatenate([rows[k:k + 1] for k in range(8)], axis=1)
            values = values * mask
            rows = jnp.concatenate(pieces(values) + [jnp.zeros_like(values)], axis=0).astype(BF16)
            tw[pl.ds(pl.multiple_of(c * 32, 32), 32), place] = rows
            return carry

        lax.fori_loop(0, COUNT // 1024, slab, 0)
        keep(c).start()

    def z_back(c, carry):
        send(True, s3, lambda place: mixed_ref.at[band(c), place], c, send4, recv4)
        return carry

    def step(c, carry):
        plane_out(c)
        plane_back(c - 1)
        core_out(c - 2)
        last(c - 2)
        return carry

    def early(c, carry):
        step(c, carry)
        z_back(c - 2, carry)
        return carry

    plane_out(0)
    plane_out(1)
    plane_back(0)
    lax.fori_loop(2, AHEAD + 2, early, 0)
    lax.fori_loop(AHEAD + 2, CHUNKS, step, 0)
    plane_back(CHUNKS - 1)
    core_out(CHUNKS - 2)
    last(CHUNKS - 2)
    core_out(CHUNKS - 1)
    last(CHUNKS - 1)

    def product(i, total):
        part = tw[:, lanes(i * 2048, 2048)]
        return total + lax.dot_general(part, part, NT, preferred_element_type=F32)

    total = lax.fori_loop(0, COUNT // 2048, product, jnp.zeros((256, 256), F32))
    rows = []
    for c in range(CHUNKS):
        part = total[32 * c:32 * c + 24]
        rows.append(part[:8] + (part[8:16] + part[16:]))
    rows = jnp.concatenate(rows, axis=0)
    lane = lax.broadcasted_iota(jnp.int32, (256, 128), 0)
    column = lax.broadcasted_iota(jnp.int32, (256, 128), 1)
    chosen = jnp.where((lane // 32) * 8 + lane % 8 == column, 1.0, 0.0)
    g_own[...] = jnp.dot(rows, chosen, precision=lax.Precision.HIGHEST, preferred_element_type=F32)

    for peer, place in zip(z_peers, z_index):
        pltpu.make_async_remote_copy(
            src_ref=g_own.at[band(place)], dst_ref=g_z.at[z], send_sem=send_gz.at[0],
            recv_sem=recv_gz.at[0], device_id=peer, device_id_type=MESH,
        ).start()
    z_back(AHEAD, 0)
    z_back(AHEAD + 1, 0)
    g_z[z] = g_own[band(z)]
    others = g_z.at[pl.ds(0, N_Z - 1)]
    pltpu.make_async_copy(others, others, recv_gz.at[0]).wait()
    g_zsum[...] = functools.reduce(lambda a, b: a + b, [g_z[k] for k in range(N_Z)])
    for peer in xy_peers:
        pltpu.make_async_remote_copy(
            src_ref=g_zsum, dst_ref=g_plane.at[q], send_sem=send_gp.at[0],
            recv_sem=recv_gp.at[0], device_id=peer, device_id_type=MESH,
        ).start()
    g_plane[q] = g_zsum[...]
    planes = g_plane.at[pl.ds(0, PLANE - 1)]
    pltpu.make_async_copy(planes, planes, recv_gp.at[0]).wait()
    g_psum[...] = functools.reduce(lambda a, b: a + b, [g_plane[k] for k in range(PLANE)])
    to_sibling = pltpu.make_async_remote_copy(
        src_ref=g_psum, dst_ref=g_core, send_sem=send_gc.at[0],
        recv_sem=recv_gc.at[0], device_id=sibling, device_id_type=MESH,
    )
    to_sibling.start()
    to_sibling.wait()
    gram[band(z)] = g_psum[...] + g_core[...]
    for peer in z_peers:
        pltpu.make_async_remote_copy(
            src_ref=gram.at[band(z)], dst_ref=gram.at[band(z)], send_sem=send_gg.at[0],
            recv_sem=recv_gg.at[0], device_id=peer, device_id_type=MESH,
        ).start()
    lax.fori_loop(AHEAD + 2, CHUNKS, z_back, 0)
    bands = gram.at[pl.ds(0, COLS - GROUP)]
    pltpu.make_async_copy(bands, bands, recv_gg.at[0]).wait()

    row = lax.broadcasted_iota(jnp.int32, (COLS, 2 * COLS), 0)
    column = lax.broadcasted_iota(jnp.int32, (COLS, 2 * COLS), 1)
    start = jnp.where(
        column < COLS, gram[...] * scale, jnp.where(column - COLS == row, 1.0, 0.0)
    )

    def eliminate(k, values):
        line = jnp.sum(jnp.where(row == k, values, 0.0), axis=0, keepdims=True)
        factor = jnp.sum(jnp.where((column == k) & (row > k), values, 0.0), axis=1, keepdims=True)
        pivot = jnp.sum(jnp.where(column[:1] == k, line, 0.0), axis=1, keepdims=True)
        return values - factor * (line / pivot)

    done = lax.fori_loop(0, COLS, eliminate, start)
    diagonal = jnp.sum(jnp.where(row == column, done, 0.0), axis=1, keepdims=True)
    done = done / jnp.sqrt(diagonal)
    square = done[:, :COLS]
    r_ref[...] = jnp.where(row[:, :COLS] <= column[:, :COLS], square * (1.0 / root), 0.0)
    inverse = done[:, COLS:] * root
    high, middle, low = [piece.astype(BF16) for piece in pieces(inverse)]
    left = jnp.concatenate([high, high, middle, high, middle, low], axis=1)

    def multiply(i, carry):
        place = lanes(i * 1024, 1024)
        values = jnp.concatenate([panel[c, :, place] for c in range(CHUNKS)], axis=0)
        high, middle, low = [piece.astype(BF16) for piece in pieces(values)]
        right = jnp.concatenate([high, middle, high, low, middle, high], axis=0)
        out[:, place] = jnp.dot(left, right, preferred_element_type=F32)
        return carry

    lax.fori_loop(0, COUNT // 1024, multiply, 0)

    pltpu.make_async_copy(others, others, send_gz.at[0]).wait()
    pltpu.make_async_copy(planes, planes, send_gp.at[0]).wait()
    pltpu.make_async_copy(bands, bands, send_gg.at[0]).wait()

    def left_all(c, carry):
        await_bytes(True, s0, c, send1)
        await_bytes(False, s1, c, send2)
        await_bytes(False, s2, c, send3)
        core_copy(c).wait_send()
        keep(c).wait()
        return carry

    lax.fori_loop(0, CHUNKS, left_all, 0)

    def arrived(c, carry):
        await_bytes(True, s3, c, send4)
        part = mixed_ref.at[band(c), pl.ds(0, COUNT - Z_LEN)]
        pltpu.make_async_copy(part, part, recv4.at[c]).wait()
        return carry

    lax.fori_loop(0, CHUNKS, arrived, 0)


def move_kernel(mixed_in, r_in, precond_in, mixed_ref, r_ref, precond_ref, sem):
    pairs = [(mixed_in, mixed_ref), (precond_in, precond_ref), (r_in, r_ref)]
    copies = [pltpu.make_async_copy(a, b, sem.at[i]) for i, (a, b) in enumerate(pairs)]
    for copy in copies:
        copy.start()
    for copy in copies:
        copy.wait()


def body(panel, signs, sample_rows):
    cols, count = panel.shape
    total = count * lax.axis_size("wide") * lax.axis_size("narrow")
    root = math.sqrt(total)
    any_space = pl.BlockSpec(memory_space=pl.ANY)
    vmem = pl.BlockSpec(memory_space=pltpu.VMEM)
    chunked = pltpu.VMEM((CHUNKS, GROUP, count), F32)
    small = pltpu.VMEM((GROUP, 128), F32)
    dma = pltpu.SemaphoreType.DMA
    shapes = [(cols, count), (cols, cols), (cols, count)]
    arguments = (panel, signs.reshape(1, count), sample_rows.reshape(-1, 128))
    results = pl.pallas_call(
        functools.partial(mix_kernel, total / sample_rows.shape[0], root),
        out_shape=tuple(pltpu.VMEM(shape, F32) for shape in shapes),
        in_specs=[any_space] * 3,
        out_specs=(vmem,) * 3,
        scratch_shapes=[
            chunked,
            pltpu.VMEM((1, count), jnp.int32),
            pltpu.VMEM((128, 128), jnp.int32),
            pltpu.VMEM((INNER, INNER), BF16),
        ]
        + [chunked] * 8
        + [
            pltpu.VMEM((4 * cols, count), BF16),
            pltpu.VMEM((128, 128), F32),
            pltpu.VMEM((cols, 128), F32),
            pltpu.VMEM((N_Z, GROUP, 128), F32),
            small,
            pltpu.VMEM((PLANE, GROUP, 128), F32),
            small,
            small,
            pltpu.VMEM((cols, 128), F32),
        ]
        + [dma((CHUNKS,))] * 2
        + [dma, dma]
        + [dma((CHUNKS,))] * 10
        + [dma((1,))] * 8
        + [pltpu.SemaphoreType.REGULAR] * 2,
        compiler_params=pltpu.CompilerParams(
            collective_id=0, has_side_effects=True, vmem_limit_bytes=48 * 1024 * 1024
        ),
    )(*(pltpu.with_memory_space_constraint(one, pltpu.HBM) for one in arguments))
    return pl.pallas_call(
        move_kernel,
        out_shape=tuple(jax.ShapeDtypeStruct(shape, F32) for shape in shapes),
        in_specs=[any_space] * 3,
        out_specs=(any_space,) * 3,
        scratch_shapes=[dma((3,))],
        compiler_params=pltpu.CompilerParams(vmem_limit_bytes=1024 * 1024),
    )(*results)


def solution(mesh):
    in_specs = (P(None, ("wide", "narrow")), P(("wide", "narrow")), P())
    out_specs = (P(None, ("wide", "narrow")), P(), P(None, ("wide", "narrow")))
    return jax.shard_map(body, mesh=mesh, in_specs=in_specs, out_specs=out_specs, check_vma=False)
```

```python
import functools
import math

import jax
import jax.numpy as jnp
from jax import lax
from jax.experimental import pallas as pl
from jax.experimental.pallas import tpu as pltpu
from jax.sharding import PartitionSpec as P

MESH = pl.DeviceIdType.MESH
F32 = jnp.float32
BF16 = jnp.bfloat16
NT = (((1,), (1,)), ((), ()))

N_Y, N_X, N_CORE, N_Z = 4, 4, 2, 8
PLANE = N_Y * N_X
COLS = 64
COUNT = 16384
GROUP = 8
CHUNKS = COLS // GROUP
DESK, TELLER = 6, 5
AHEAD = 4
Z_LEN = COUNT // N_Z
P_LEN = COUNT // PLANE
INNER = 256


def butterflies(parts):
    parts = list(parts)
    half = 1
    while half < len(parts):
        for low in range(len(parts)):
            if not low & half:
                first, second = parts[low], parts[low | half]
                parts[low], parts[low | half] = first + second, first - second
        half *= 2
    return parts


def pieces(values):
    high = values.astype(BF16).astype(F32)
    rest = values - high
    middle = rest.astype(BF16).astype(F32)
    return [high, middle, rest - middle]


def lanes(start, size):
    return pl.ds(pl.multiple_of(start, 128), size)


def device(y, x, core, z):
    return (((y % N_Y) * N_X + x % N_X) * N_CORE + core % N_CORE, z % N_Z)


def mix_kernel(
    scale, root, panel_ref, signs_hbm, samples_hbm, mixed_ref, r_ref, out,
    panel, signs_ref, samples_ref, h_ref, s0, r1, s1, r2, s2, r3, e, s3, tw, weight,
    g_own, g_z, g_zsum, g_plane, g_core, gram,
    in_sem, own_sem, signs_sem, samples_sem, send1, recv1, send2, recv2, send3, recv3, send4, recv4,
    send_core, recv_core, send_gz, recv_gz, send_gp, recv_gp, send_gc, recv_gc,
    send_gg, recv_gg, ring_sem, plane_sem,
):
    wide = lax.axis_index("wide")
    z = lax.axis_index("narrow")
    core = wide % N_CORE
    x = (wide // N_CORE) % N_X
    y = wide // (N_CORE * N_X)
    q = wide // N_CORE
    z_peers = [device(y, x, core, z + d) for d in range(1, N_Z)]
    z_index = [(z + d) % N_Z for d in range(1, N_Z)]
    xy_offsets = [(a, b) for a in range(N_Y) for b in range(N_X) if a or b]
    xy_peers = [device(y + a, x + b, core, z) for a, b in xy_offsets]
    xy_index = [((y + a) % N_Y) * N_X + (x + b) % N_X for a, b in xy_offsets]
    sibling = device(y, x, core + 1, z)

    def band(c):
        return pl.ds(pl.multiple_of(c * GROUP, GROUP), GROUP)

    def load(c):
        return pltpu.make_async_copy(panel_ref.at[band(c)], panel.at[c], in_sem.at[c])

    barrier = pltpu.get_barrier_semaphore()

    def greet(some):
        for peer in some:
            pl.semaphore_signal(barrier, inc=1, device_id=peer, device_id_type=MESH)

    load_signs = pltpu.make_async_copy(signs_hbm, signs_ref, signs_sem)
    load_samples = pltpu.make_async_copy(samples_hbm, samples_ref, samples_sem)
    for d in range(1, N_Z):
        pl.when((z + d) % N_Z != DESK)(functools.partial(greet, [z_peers[d - 1]]))
    load_signs.start()
    load(0).start()

    @pl.when(z == TELLER)
    def _():
        pl.semaphore_wait(barrier, N_Z - 1)
        pl.semaphore_signal(
            ring_sem, inc=1, device_id=device(y, x, core, DESK), device_id_type=MESH
        )

    for c in range(1, CHUNKS):
        load(c).start()
    load_samples.start()

    def send(over_z, src, target, c, send_sem, recv_sem):
        size = Z_LEN if over_z else P_LEN
        peers, index = (z_peers, z_index) if over_z else (xy_peers, xy_index)
        for peer, place in zip(peers, index):
            pltpu.make_async_remote_copy(
                src_ref=src.at[c, :, lanes(place * size, size)],
                dst_ref=target(lanes((z if over_z else q) * size, size)),
                send_sem=send_sem.at[c],
                recv_sem=recv_sem.at[c],
                device_id=peer,
                device_id_type=MESH,
            ).start()

    def await_bytes(over_z, ref, c, sem):
        part = ref.at[c, :, pl.ds(0, COUNT - (Z_LEN if over_z else P_LEN))]
        pltpu.make_async_copy(part, part, sem.at[c]).wait()

    def mix(c):
        load(c).wait()

        def part(i, carry):
            places = [lanes(p * Z_LEN + i * 512, 512) for p in range(N_Z)]
            values = [panel[c, :, place] * signs_ref[:, place].astype(F32) for place in places]
            for place, value in zip(places, butterflies(values)):
                s0[c, :, place] = value
            return carry

        lax.fori_loop(0, Z_LEN // 512, part, 0)

    def send_z(c):
        send(True, s0, lambda place: r1.at[c, :, place], c, send1, recv1)

    load_signs.wait()
    mix(0)

    @pl.when((z != TELLER) & (z != DESK))
    def _():
        pl.semaphore_wait(barrier, N_Z - 1)

    @pl.when(z == DESK)
    def _():
        pl.semaphore_wait(ring_sem, 1)

    send_z(0)

    @pl.when(z == DESK)
    def _():
        greet(xy_peers + [sibling])


    def begin(c, carry):
        mix(c)
        send_z(c)
        return carry

    lax.fori_loop(1, CHUNKS, begin, 0)

    load_samples.wait()
    weight[...] = jnp.zeros_like(weight)

    def mark(i, carry):
        rows = samples_ref[pl.ds(pl.multiple_of(i * 8, 8), 8), :]
        offsets = rows - wide * (N_Z * COUNT)
        place = jnp.bitwise_and(jnp.right_shift(offsets, 11), N_Z - 1)
        inside = (jnp.right_shift(offsets, 17) == 0) & (place == z)
        inner = jnp.bitwise_and(jnp.right_shift(offsets, 7), Z_LEN // 128 - 1)
        high = jnp.where(inside, jnp.right_shift(offsets, 14) * (Z_LEN // 128) + inner, -1)
        low = jnp.bitwise_and(offsets, 127)
        places = lax.broadcasted_iota(jnp.int32, (128, 128), 0)
        total = jnp.zeros((128, 128), F32)
        for r in range(0, 8, 2):
            above = [jnp.where(places == high[k:k + 1], 1.0, 0.0) for k in (r, r + 1)]
            below = [jnp.where(places == low[k:k + 1], 1.0, 0.0) for k in (r, r + 1)]
            total += lax.dot_general(
                jnp.concatenate(above, axis=1).astype(BF16),
                jnp.concatenate(below, axis=1).astype(BF16),
                NT,
                preferred_element_type=F32,
            )
        weight[...] += total
        return carry

    lax.fori_loop(0, 16, mark, 0)

    @pl.when(z == DESK)
    def _():
        pl.semaphore_wait(barrier, PLANE)
        for peer in z_peers:
            pl.semaphore_signal(plane_sem, inc=1, device_id=peer, device_id_type=MESH)

    @pl.when(z != DESK)
    def _():
        pl.semaphore_wait(plane_sem, 1)

    common = jnp.bitwise_and(
        lax.broadcasted_iota(jnp.int32, (INNER, INNER), 0),
        lax.broadcasted_iota(jnp.int32, (INNER, INNER), 1),
    )
    for shift in (4, 2, 1):
        common = jnp.bitwise_xor(common, jnp.right_shift(common, shift))
    h_ref[...] = jnp.where(jnp.bitwise_and(common, 1) == 0, 1.0 / root, -1.0 / root).astype(BF16)

    def plane_out(c):
        await_bytes(True, r1, c, recv1)
        mine = lanes(z * Z_LEN, Z_LEN)
        r1[c, :, mine] = s0[c, :, mine]

        def inner(i, carry):
            places = [lanes(p * Z_LEN + i * INNER, INNER) for p in range(N_Z)]
            values = butterflies([r1[c, :, place] for place in places])
            rows = []
            for value in values:
                rows += pieces(value)
            stacked = jnp.concatenate(rows, axis=0).astype(BF16)
            done = jnp.dot(stacked, h_ref[...], preferred_element_type=F32)
            for p, place in enumerate(places):
                part = done[24 * p:24 * p + 24]
                s1[c, :, place] = part[:8] + (part[8:16] + part[16:])
            return carry

        lax.fori_loop(0, Z_LEN // INNER, inner, 0)

        def outer(p, carry):
            places = [lanes(p * Z_LEN + i * INNER, INNER) for i in range(Z_LEN // INNER)]
            values = butterflies([s1[c, :, place] for place in places])
            for place, value in zip(places, values):
                s1[c, :, place] = value
            return carry

        lax.fori_loop(0, N_Z, outer, 0)
        send(False, s1, lambda place: r2.at[c, :, place], c, send2, recv2)

    def plane_back(c):
        await_bytes(False, r2, c, recv2)
        mine = lanes(q * P_LEN, P_LEN)
        r2[c, :, mine] = s1[c, :, mine]

        def part(i, carry):
            places = [lanes(p * P_LEN + i * 256, 256) for p in range(PLANE)]
            values = butterflies([r2[c, :, place] for place in places])
            for place, value in zip(places, values):
                s2[c, :, place] = value
            return carry

        lax.fori_loop(0, P_LEN // 256, part, 0)
        send(False, s2, lambda place: r3.at[c, :, place], c, send3, recv3)

    def core_copy(c):
        return pltpu.make_async_remote_copy(
            src_ref=r3.at[c], dst_ref=e.at[c], send_sem=send_core.at[c], recv_sem=recv_core.at[c],
            device_id=sibling, device_id_type=MESH,
        )

    def core_out(c):
        await_bytes(False, r3, c, recv3)
        mine = lanes(q * P_LEN, P_LEN)
        r3[c, :, mine] = s2[c, :, mine]
        core_copy(c).start()

    flip = 1.0 - 2.0 * core.astype(F32)

    def keep(c):
        mine = lanes(z * Z_LEN, Z_LEN)
        return pltpu.make_async_copy(s3.at[c, :, mine], mixed_ref.at[band(c), mine], own_sem.at[c])

    def last(c):
        core_copy(c).wait_recv()

        def slab(i, carry):
            place = lanes(i * 1024, 1024)
            values = e[c, :, place] + flip * r3[c, :, place]
            s3[c, :, place] = values
            rows = weight[pl.ds(pl.multiple_of(i * 8, 8), 8), :]
            mask = jnp.concatenate([rows[k:k + 1] for k in range(8)], axis=1)
            values = values * mask
            rows = jnp.concatenate(pieces(values) + [jnp.zeros_like(values)], axis=0).astype(BF16)
            tw[pl.ds(pl.multiple_of(c * 32, 32), 32), place] = rows
            return carry

        lax.fori_loop(0, COUNT // 1024, slab, 0)
        keep(c).start()

    def z_back(c, carry):
        send(True, s3, lambda place: mixed_ref.at[band(c), place], c, send4, recv4)
        return carry

    def step(c, carry):
        plane_out(c)
        plane_back(c - 1)
        core_out(c - 2)
        last(c - 2)
        return carry

    def early(c, carry):
        step(c, carry)
        z_back(c - 2, carry)
        return carry

    plane_out(0)
    plane_out(1)
    plane_back(0)
    lax.fori_loop(2, AHEAD + 2, early, 0)
    lax.fori_loop(AHEAD + 2, CHUNKS, step, 0)
    plane_back(CHUNKS - 1)
    core_out(CHUNKS - 2)
    last(CHUNKS - 2)
    core_out(CHUNKS - 1)
    last(CHUNKS - 1)

    def product(i, total):
        part = tw[:, lanes(i * 2048, 2048)]
        return total + lax.dot_general(part, part, NT, preferred_element_type=F32)

    total = lax.fori_loop(0, COUNT // 2048, product, jnp.zeros((256, 256), F32))
    rows = []
    for c in range(CHUNKS):
        part = total[32 * c:32 * c + 24]
        rows.append(part[:8] + (part[8:16] + part[16:]))
    rows = jnp.concatenate(rows, axis=0)
    lane = lax.broadcasted_iota(jnp.int32, (256, 128), 0)
    column = lax.broadcasted_iota(jnp.int32, (256, 128), 1)
    chosen = jnp.where((lane // 32) * 8 + lane % 8 == column, 1.0, 0.0)
    g_own[...] = jnp.dot(rows, chosen, precision=lax.Precision.HIGHEST, preferred_element_type=F32)

    def to_sibling(src, dst, i):
        return pltpu.make_async_remote_copy(
            src_ref=src, dst_ref=dst, send_sem=send_gc.at[i], recv_sem=recv_gc.at[i],
            device_id=sibling, device_id_type=MESH,
        )

    others = g_z.at[pl.ds(0, N_Z - 1)]
    planes = g_plane.at[pl.ds(0, PLANE - 1)]
    bands = gram.at[pl.ds(0, COLS - GROUP)]

    @pl.when(core == 1)
    def _():
        to_sibling(g_own, g_core, 0).start()

    @pl.when(core == 0)
    def _():
        to_sibling(g_own, g_core, 0).wait_recv()
        g_own[...] += g_core[...]
        for peer, place in zip(z_peers, z_index):
            pltpu.make_async_remote_copy(
                src_ref=g_own.at[band(place)], dst_ref=g_z.at[z], send_sem=send_gz.at[0],
                recv_sem=recv_gz.at[0], device_id=peer, device_id_type=MESH,
            ).start()

    z_back(AHEAD, 0)
    z_back(AHEAD + 1, 0)

    @pl.when(core == 0)
    def _():
        g_z[z] = g_own[band(z)]
        pltpu.make_async_copy(others, others, recv_gz.at[0]).wait()
        g_zsum[...] = functools.reduce(lambda a, b: a + b, [g_z[k] for k in range(N_Z)])
        for peer in xy_peers:
            pltpu.make_async_remote_copy(
                src_ref=g_zsum, dst_ref=g_plane.at[q], send_sem=send_gp.at[0],
                recv_sem=recv_gp.at[0], device_id=peer, device_id_type=MESH,
            ).start()
        g_plane[q] = g_zsum[...]
        pltpu.make_async_copy(planes, planes, recv_gp.at[0]).wait()
        gram[band(z)] = functools.reduce(lambda a, b: a + b, [g_plane[k] for k in range(PLANE)])
        for peer in z_peers:
            pltpu.make_async_remote_copy(
                src_ref=gram.at[band(z)], dst_ref=gram.at[band(z)], send_sem=send_gg.at[0],
                recv_sem=recv_gg.at[0], device_id=peer, device_id_type=MESH,
            ).start()

    lax.fori_loop(AHEAD + 2, CHUNKS, z_back, 0)

    @pl.when(core == 0)
    def _():
        pltpu.make_async_copy(bands, bands, recv_gg.at[0]).wait()
        to_sibling(gram, gram, 1).start()

    @pl.when(core == 1)
    def _():
        to_sibling(gram, gram, 1).wait_recv()

    row = lax.broadcasted_iota(jnp.int32, (COLS, 2 * COLS), 0)
    column = lax.broadcasted_iota(jnp.int32, (COLS, 2 * COLS), 1)
    start = jnp.where(
        column < COLS, gram[...] * scale, jnp.where(column - COLS == row, 1.0, 0.0)
    )

    def eliminate(k, values):
        line = jnp.sum(jnp.where(row == k, values, 0.0), axis=0, keepdims=True)
        factor = jnp.sum(jnp.where((column == k) & (row > k), values, 0.0), axis=1, keepdims=True)
        pivot = jnp.sum(jnp.where(column[:1] == k, line, 0.0), axis=1, keepdims=True)
        return values - factor * (line / pivot)

    done = lax.fori_loop(0, COLS, eliminate, start)
    diagonal = jnp.sum(jnp.where(row == column, done, 0.0), axis=1, keepdims=True)
    done = done / jnp.sqrt(diagonal)
    square = done[:, :COLS]
    r_ref[...] = jnp.where(row[:, :COLS] <= column[:, :COLS], square * (1.0 / root), 0.0)
    inverse = done[:, COLS:] * root
    high, middle, low = [piece.astype(BF16) for piece in pieces(inverse)]
    left = jnp.concatenate([high, high, middle, high, middle, low], axis=1)

    def multiply(i, carry):
        place = lanes(i * 1024, 1024)
        values = jnp.concatenate([panel[c, :, place] for c in range(CHUNKS)], axis=0)
        high, middle, low = [piece.astype(BF16) for piece in pieces(values)]
        right = jnp.concatenate([high, middle, high, low, middle, high], axis=0)
        out[:, place] = jnp.dot(left, right, preferred_element_type=F32)
        return carry

    lax.fori_loop(0, COUNT // 1024, multiply, 0)

    @pl.when(core == 0)
    def _():
        pltpu.make_async_copy(others, others, send_gz.at[0]).wait()
        pltpu.make_async_copy(planes, planes, send_gp.at[0]).wait()
        pltpu.make_async_copy(bands, bands, send_gg.at[0]).wait()
        to_sibling(gram, gram, 1).wait_send()

    @pl.when(core == 1)
    def _():
        to_sibling(g_own, g_core, 0).wait_send()


    def left_all(c, carry):
        await_bytes(True, s0, c, send1)
        await_bytes(False, s1, c, send2)
        await_bytes(False, s2, c, send3)
        core_copy(c).wait_send()
        keep(c).wait()
        return carry

    lax.fori_loop(0, CHUNKS, left_all, 0)

    def arrived(c, carry):
        await_bytes(True, s3, c, send4)
        part = mixed_ref.at[band(c), pl.ds(0, COUNT - Z_LEN)]
        pltpu.make_async_copy(part, part, recv4.at[c]).wait()
        return carry

    lax.fori_loop(0, CHUNKS, arrived, 0)


def move_kernel(mixed_in, r_in, precond_in, mixed_ref, r_ref, precond_ref, sem):
    pairs = [(mixed_in, mixed_ref), (precond_in, precond_ref), (r_in, r_ref)]
    copies = [pltpu.make_async_copy(a, b, sem.at[i]) for i, (a, b) in enumerate(pairs)]
    for copy in copies:
        copy.start()
    for copy in copies:
        copy.wait()


def body(panel, signs, sample_rows):
    cols, count = panel.shape
    total = count * lax.axis_size("wide") * lax.axis_size("narrow")
    root = math.sqrt(total)
    any_space = pl.BlockSpec(memory_space=pl.ANY)
    vmem = pl.BlockSpec(memory_space=pltpu.VMEM)
    chunked = pltpu.VMEM((CHUNKS, GROUP, count), F32)
    small = pltpu.VMEM((GROUP, 128), F32)
    dma = pltpu.SemaphoreType.DMA
    shapes = [(cols, count), (cols, cols), (cols, count)]
    arguments = (panel, signs.reshape(1, count), sample_rows.reshape(-1, 128))
    results = pl.pallas_call(
        functools.partial(mix_kernel, total / sample_rows.shape[0], root),
        out_shape=tuple(pltpu.VMEM(shape, F32) for shape in shapes),
        in_specs=[any_space] * 3,
        out_specs=(vmem,) * 3,
        scratch_shapes=[
            chunked,
            pltpu.VMEM((1, count), jnp.int32),
            pltpu.VMEM((128, 128), jnp.int32),
            pltpu.VMEM((INNER, INNER), BF16),
        ]
        + [chunked] * 8
        + [
            pltpu.VMEM((4 * cols, count), BF16),
            pltpu.VMEM((128, 128), F32),
            pltpu.VMEM((cols, 128), F32),
            pltpu.VMEM((N_Z, GROUP, 128), F32),
            small,
            pltpu.VMEM((PLANE, GROUP, 128), F32),
            pltpu.VMEM((cols, 128), F32),
            pltpu.VMEM((cols, 128), F32),
        ]
        + [dma((CHUNKS,))] * 2
        + [dma, dma]
        + [dma((CHUNKS,))] * 10
        + [dma((1,))] * 4
        + [dma((2,))] * 2
        + [dma((1,))] * 2
        + [pltpu.SemaphoreType.REGULAR] * 2,
        compiler_params=pltpu.CompilerParams(
            collective_id=0, has_side_effects=True, vmem_limit_bytes=48 * 1024 * 1024
        ),
    )(*(pltpu.with_memory_space_constraint(one, pltpu.HBM) for one in arguments))
    return pl.pallas_call(
        move_kernel,
        out_shape=tuple(jax.ShapeDtypeStruct(shape, F32) for shape in shapes),
        in_specs=[any_space] * 3,
        out_specs=(any_space,) * 3,
        scratch_shapes=[dma((3,))],
        compiler_params=pltpu.CompilerParams(vmem_limit_bytes=1024 * 1024),
    )(*results)


def solution(mesh):
    in_specs = (P(None, ("wide", "narrow")), P(("wide", "narrow")), P())
    out_specs = (P(None, ("wide", "narrow")), P(), P(None, ("wide", "narrow")))
    return jax.shard_map(body, mesh=mesh, in_specs=in_specs, out_specs=out_specs, check_vma=False)
```

```python
import functools
import math

import jax
import jax.numpy as jnp
from jax import lax
from jax.experimental import pallas as pl
from jax.experimental.pallas import tpu as pltpu
from jax.sharding import PartitionSpec as P

MESH = pl.DeviceIdType.MESH
F32 = jnp.float32
BF16 = jnp.bfloat16
NT = (((1,), (1,)), ((), ()))

N_Y, N_X, N_CORE, N_Z = 4, 4, 2, 8
PLANE = N_Y * N_X
COLS = 64
COUNT = 16384
GROUP = 8
CHUNKS = COLS // GROUP
DESK, TELLER = 6, 5
AHEAD = 3
Z_LEN = COUNT // N_Z
P_LEN = COUNT // PLANE
INNER = 256


def butterflies(parts):
    parts = list(parts)
    half = 1
    while half < len(parts):
        for low in range(len(parts)):
            if not low & half:
                first, second = parts[low], parts[low | half]
                parts[low], parts[low | half] = first + second, first - second
        half *= 2
    return parts


def pieces(values):
    high = values.astype(BF16).astype(F32)
    rest = values - high
    middle = rest.astype(BF16).astype(F32)
    return [high, middle, rest - middle]


def lanes(start, size):
    return pl.ds(pl.multiple_of(start, 128), size)


def device(y, x, core, z):
    return (((y % N_Y) * N_X + x % N_X) * N_CORE + core % N_CORE, z % N_Z)


def mix_kernel(
    scale, root, panel_ref, signs_hbm, samples_hbm, mixed_ref, r_ref, out,
    panel, signs_ref, samples_ref, h_ref, s0, r1, s1, r2, s2, r3, e, s3, tw, weight,
    g_own, g_z, g_zsum, g_plane, g_core, gram,
    in_sem, own_sem, signs_sem, samples_sem, send1, recv1, send2, recv2, send3, recv3, send4, recv4,
    send_core, recv_core, send_gz, recv_gz, send_gp, recv_gp, send_gc, recv_gc,
    send_gg, recv_gg, ring_sem, plane_sem,
):
    wide = lax.axis_index("wide")
    z = lax.axis_index("narrow")
    core = wide % N_CORE
    x = (wide // N_CORE) % N_X
    y = wide // (N_CORE * N_X)
    q = wide // N_CORE
    z_peers = [device(y, x, core, z + d) for d in range(1, N_Z)]
    z_index = [(z + d) % N_Z for d in range(1, N_Z)]
    xy_offsets = [(a, b) for a in range(N_Y) for b in range(N_X) if a or b]
    xy_peers = [device(y + a, x + b, core, z) for a, b in xy_offsets]
    xy_index = [((y + a) % N_Y) * N_X + (x + b) % N_X for a, b in xy_offsets]
    sibling = device(y, x, core + 1, z)

    def band(c):
        return pl.ds(pl.multiple_of(c * GROUP, GROUP), GROUP)

    def load(c):
        return pltpu.make_async_copy(panel_ref.at[band(c)], panel.at[c], in_sem.at[c])

    barrier = pltpu.get_barrier_semaphore()

    def greet(some):
        for peer in some:
            pl.semaphore_signal(barrier, inc=1, device_id=peer, device_id_type=MESH)

    load_signs = pltpu.make_async_copy(signs_hbm, signs_ref, signs_sem)
    load_samples = pltpu.make_async_copy(samples_hbm, samples_ref, samples_sem)
    load_signs.start()
    load(0).start()
    for d in range(1, N_Z):
        pl.when((z + d) % N_Z != DESK)(functools.partial(greet, [z_peers[d - 1]]))

    @pl.when(z == TELLER)
    def _():
        pl.semaphore_wait(barrier, N_Z - 1)
        pl.semaphore_signal(
            ring_sem, inc=1, device_id=device(y, x, core, DESK), device_id_type=MESH
        )

    for c in range(1, CHUNKS):
        load(c).start()
    load_samples.start()

    def send(over_z, src, target, c, send_sem, recv_sem):
        size = Z_LEN if over_z else P_LEN
        peers, index = (z_peers, z_index) if over_z else (xy_peers, xy_index)
        for peer, place in zip(peers, index):
            pltpu.make_async_remote_copy(
                src_ref=src.at[c, :, lanes(place * size, size)],
                dst_ref=target(lanes((z if over_z else q) * size, size)),
                send_sem=send_sem.at[c],
                recv_sem=recv_sem.at[c],
                device_id=peer,
                device_id_type=MESH,
            ).start()

    def await_bytes(over_z, ref, c, sem):
        part = ref.at[c, :, pl.ds(0, COUNT - (Z_LEN if over_z else P_LEN))]
        pltpu.make_async_copy(part, part, sem.at[c]).wait()

    def mix(c):
        load(c).wait()

        def part(i, carry):
            places = [lanes(p * Z_LEN + i * 512, 512) for p in range(N_Z)]
            values = [panel[c, :, place] * signs_ref[:, place].astype(F32) for place in places]
            for place, value in zip(places, butterflies(values)):
                s0[c, :, place] = value
            return carry

        lax.fori_loop(0, Z_LEN // 512, part, 0)

    def send_z(c):
        send(True, s0, lambda place: r1.at[c, :, place], c, send1, recv1)

    load_signs.wait()
    mix(0)

    @pl.when((z != TELLER) & (z != DESK))
    def _():
        pl.semaphore_wait(barrier, N_Z - 1)

    @pl.when(z == DESK)
    def _():
        pl.semaphore_wait(ring_sem, 1)

    send_z(0)

    @pl.when(z == DESK)
    def _():
        greet(xy_peers + [sibling])


    def begin(c, carry):
        mix(c)
        send_z(c)
        return carry

    lax.fori_loop(1, CHUNKS, begin, 0)

    load_samples.wait()
    weight[...] = jnp.zeros_like(weight)

    def mark(i, carry):
        rows = samples_ref[pl.ds(pl.multiple_of(i * 8, 8), 8), :]
        offsets = rows - wide * (N_Z * COUNT)
        place = jnp.bitwise_and(jnp.right_shift(offsets, 11), N_Z - 1)
        inside = (jnp.right_shift(offsets, 17) == 0) & (place == z)
        inner = jnp.bitwise_and(jnp.right_shift(offsets, 7), Z_LEN // 128 - 1)
        high = jnp.where(inside, jnp.right_shift(offsets, 14) * (Z_LEN // 128) + inner, -1)
        low = jnp.bitwise_and(offsets, 127)
        places = lax.broadcasted_iota(jnp.int32, (128, 128), 0)
        total = jnp.zeros((128, 128), F32)
        for r in range(0, 8, 2):
            above = [jnp.where(places == high[k:k + 1], 1.0, 0.0) for k in (r, r + 1)]
            below = [jnp.where(places == low[k:k + 1], 1.0, 0.0) for k in (r, r + 1)]
            total += lax.dot_general(
                jnp.concatenate(above, axis=1).astype(BF16),
                jnp.concatenate(below, axis=1).astype(BF16),
                NT,
                preferred_element_type=F32,
            )
        weight[...] += total
        return carry

    lax.fori_loop(0, 16, mark, 0)

    @pl.when(z == DESK)
    def _():
        pl.semaphore_wait(barrier, PLANE)
        for peer in z_peers:
            pl.semaphore_signal(plane_sem, inc=1, device_id=peer, device_id_type=MESH)

    @pl.when(z != DESK)
    def _():
        pl.semaphore_wait(plane_sem, 1)

    common = jnp.bitwise_and(
        lax.broadcasted_iota(jnp.int32, (INNER, INNER), 0),
        lax.broadcasted_iota(jnp.int32, (INNER, INNER), 1),
    )
    for shift in (4, 2, 1):
        common = jnp.bitwise_xor(common, jnp.right_shift(common, shift))
    h_ref[...] = jnp.where(jnp.bitwise_and(common, 1) == 0, 1.0 / root, -1.0 / root).astype(BF16)

    def plane_out(c):
        await_bytes(True, r1, c, recv1)
        mine = lanes(z * Z_LEN, Z_LEN)
        r1[c, :, mine] = s0[c, :, mine]

        def inner(i, carry):
            places = [lanes(p * Z_LEN + i * INNER, INNER) for p in range(N_Z)]
            values = butterflies([r1[c, :, place] for place in places])
            rows = []
            for value in values:
                rows += pieces(value)
            stacked = jnp.concatenate(rows, axis=0).astype(BF16)
            done = jnp.dot(stacked, h_ref[...], preferred_element_type=F32)
            for p, place in enumerate(places):
                part = done[24 * p:24 * p + 24]
                s1[c, :, place] = part[:8] + (part[8:16] + part[16:])
            return carry

        lax.fori_loop(0, Z_LEN // INNER, inner, 0)

        def outer(p, carry):
            places = [lanes(p * Z_LEN + i * INNER, INNER) for i in range(Z_LEN // INNER)]
            values = butterflies([s1[c, :, place] for place in places])
            for place, value in zip(places, values):
                s1[c, :, place] = value
            return carry

        lax.fori_loop(0, N_Z, outer, 0)
        send(False, s1, lambda place: r2.at[c, :, place], c, send2, recv2)

    def plane_back(c):
        await_bytes(False, r2, c, recv2)
        mine = lanes(q * P_LEN, P_LEN)
        r2[c, :, mine] = s1[c, :, mine]

        def part(i, carry):
            places = [lanes(p * P_LEN + i * 256, 256) for p in range(PLANE)]
            values = butterflies([r2[c, :, place] for place in places])
            for place, value in zip(places, values):
                s2[c, :, place] = value
            return carry

        lax.fori_loop(0, P_LEN // 256, part, 0)
        send(False, s2, lambda place: r3.at[c, :, place], c, send3, recv3)

    def core_copy(c):
        return pltpu.make_async_remote_copy(
            src_ref=r3.at[c], dst_ref=e.at[c], send_sem=send_core.at[c], recv_sem=recv_core.at[c],
            device_id=sibling, device_id_type=MESH,
        )

    def core_out(c):
        await_bytes(False, r3, c, recv3)
        mine = lanes(q * P_LEN, P_LEN)
        r3[c, :, mine] = s2[c, :, mine]
        core_copy(c).start()

    flip = 1.0 - 2.0 * core.astype(F32)

    def keep(c):
        mine = lanes(z * Z_LEN, Z_LEN)
        return pltpu.make_async_copy(s3.at[c, :, mine], mixed_ref.at[band(c), mine], own_sem.at[c])

    def last(c):
        core_copy(c).wait_recv()

        def slab(i, carry):
            place = lanes(i * 1024, 1024)
            values = e[c, :, place] + flip * r3[c, :, place]
            s3[c, :, place] = values
            rows = weight[pl.ds(pl.multiple_of(i * 8, 8), 8), :]
            mask = jnp.concatenate([rows[k:k + 1] for k in range(8)], axis=1)
            values = values * mask
            rows = jnp.concatenate(pieces(values) + [jnp.zeros_like(values)], axis=0).astype(BF16)
            tw[pl.ds(pl.multiple_of(c * 32, 32), 32), place] = rows
            return carry

        lax.fori_loop(0, COUNT // 1024, slab, 0)
        keep(c).start()

    def z_back(c, carry):
        send(True, s3, lambda place: mixed_ref.at[band(c), place], c, send4, recv4)
        return carry

    def step(c, carry):
        plane_out(c)
        plane_back(c - 1)
        core_out(c - 2)
        last(c - 2)
        return carry

    def early(c, carry):
        step(c, carry)
        z_back(c - 2, carry)
        return carry

    plane_out(0)
    plane_out(1)
    plane_back(0)
    lax.fori_loop(2, AHEAD + 2, early, 0)
    lax.fori_loop(AHEAD + 2, CHUNKS, step, 0)
    plane_back(CHUNKS - 1)
    core_out(CHUNKS - 2)
    last(CHUNKS - 2)
    core_out(CHUNKS - 1)
    last(CHUNKS - 1)

    def product(i, total):
        part = tw[:, lanes(i * 2048, 2048)]
        return total + lax.dot_general(part, part, NT, preferred_element_type=F32)

    total = lax.fori_loop(0, COUNT // 2048, product, jnp.zeros((256, 256), F32))
    rows = []
    for c in range(CHUNKS):
        part = total[32 * c:32 * c + 24]
        rows.append(part[:8] + (part[8:16] + part[16:]))
    rows = jnp.concatenate(rows, axis=0)
    lane = lax.broadcasted_iota(jnp.int32, (256, 128), 0)
    column = lax.broadcasted_iota(jnp.int32, (256, 128), 1)
    chosen = jnp.where((lane // 32) * 8 + lane % 8 == column, 1.0, 0.0)
    g_own[...] = jnp.dot(rows, chosen, precision=lax.Precision.HIGHEST, preferred_element_type=F32)

    def to_sibling(src, dst, i):
        return pltpu.make_async_remote_copy(
            src_ref=src, dst_ref=dst, send_sem=send_gc.at[i], recv_sem=recv_gc.at[i],
            device_id=sibling, device_id_type=MESH,
        )

    others = g_z.at[pl.ds(0, N_Z - 1)]
    planes = g_plane.at[pl.ds(0, PLANE - 1)]
    bands = gram.at[pl.ds(0, COLS - GROUP)]

    @pl.when(core == 1)
    def _():
        to_sibling(g_own, g_core, 0).start()

    @pl.when(core == 0)
    def _():
        to_sibling(g_own, g_core, 0).wait_recv()
        g_own[...] += g_core[...]
        for peer, place in zip(z_peers, z_index):
            pltpu.make_async_remote_copy(
                src_ref=g_own.at[band(place)], dst_ref=g_z.at[z], send_sem=send_gz.at[0],
                recv_sem=recv_gz.at[0], device_id=peer, device_id_type=MESH,
            ).start()

    z_back(AHEAD, 0)
    z_back(AHEAD + 1, 0)

    @pl.when(core == 0)
    def _():
        g_z[z] = g_own[band(z)]
        pltpu.make_async_copy(others, others, recv_gz.at[0]).wait()
        g_zsum[...] = functools.reduce(lambda a, b: a + b, [g_z[k] for k in range(N_Z)])
        for peer in xy_peers:
            pltpu.make_async_remote_copy(
                src_ref=g_zsum, dst_ref=g_plane.at[q], send_sem=send_gp.at[0],
                recv_sem=recv_gp.at[0], device_id=peer, device_id_type=MESH,
            ).start()
        g_plane[q] = g_zsum[...]
        pltpu.make_async_copy(planes, planes, recv_gp.at[0]).wait()
        gram[band(z)] = functools.reduce(lambda a, b: a + b, [g_plane[k] for k in range(PLANE)])
        for peer in z_peers:
            pltpu.make_async_remote_copy(
                src_ref=gram.at[band(z)], dst_ref=gram.at[band(z)], send_sem=send_gg.at[0],
                recv_sem=recv_gg.at[0], device_id=peer, device_id_type=MESH,
            ).start()

    lax.fori_loop(AHEAD + 2, CHUNKS, z_back, 0)

    @pl.when(core == 0)
    def _():
        pltpu.make_async_copy(bands, bands, recv_gg.at[0]).wait()
        to_sibling(gram, gram, 1).start()

    @pl.when(core == 1)
    def _():
        to_sibling(gram, gram, 1).wait_recv()

    row = lax.broadcasted_iota(jnp.int32, (COLS, 2 * COLS), 0)
    column = lax.broadcasted_iota(jnp.int32, (COLS, 2 * COLS), 1)
    start = jnp.where(
        column < COLS, gram[...] * scale, jnp.where(column - COLS == row, 1.0, 0.0)
    )

    def eliminate(k, values):
        line = jnp.sum(jnp.where(row == k, values, 0.0), axis=0, keepdims=True)
        factor = jnp.sum(jnp.where((column == k) & (row > k), values, 0.0), axis=1, keepdims=True)
        pivot = jnp.sum(jnp.where(column[:1] == k, line, 0.0), axis=1, keepdims=True)
        return values - factor * (line / pivot)

    done = lax.fori_loop(0, COLS, eliminate, start)
    diagonal = jnp.sum(jnp.where(row == column, done, 0.0), axis=1, keepdims=True)
    done = done / jnp.sqrt(diagonal)
    square = done[:, :COLS]
    r_ref[...] = jnp.where(row[:, :COLS] <= column[:, :COLS], square * (1.0 / root), 0.0)
    inverse = done[:, COLS:] * root
    high, middle, low = [piece.astype(BF16) for piece in pieces(inverse)]
    left = jnp.concatenate([high, high, middle, high, middle, low], axis=1)

    def multiply(i, carry):
        place = lanes(i * 1024, 1024)
        values = jnp.concatenate([panel[c, :, place] for c in range(CHUNKS)], axis=0)
        high, middle, low = [piece.astype(BF16) for piece in pieces(values)]
        right = jnp.concatenate([high, middle, high, low, middle, high], axis=0)
        out[:, place] = jnp.dot(left, right, preferred_element_type=F32)
        return carry

    lax.fori_loop(0, COUNT // 1024, multiply, 0)

    @pl.when(core == 0)
    def _():
        pltpu.make_async_copy(others, others, send_gz.at[0]).wait()
        pltpu.make_async_copy(planes, planes, send_gp.at[0]).wait()
        pltpu.make_async_copy(bands, bands, send_gg.at[0]).wait()
        to_sibling(gram, gram, 1).wait_send()

    @pl.when(core == 1)
    def _():
        to_sibling(g_own, g_core, 0).wait_send()


    def left_all(c, carry):
        await_bytes(True, s0, c, send1)
        await_bytes(False, s1, c, send2)
        await_bytes(False, s2, c, send3)
        core_copy(c).wait_send()
        keep(c).wait()
        return carry

    lax.fori_loop(0, CHUNKS, left_all, 0)

    def arrived(c, carry):
        await_bytes(True, s3, c, send4)
        part = mixed_ref.at[band(c), pl.ds(0, COUNT - Z_LEN)]
        pltpu.make_async_copy(part, part, recv4.at[c]).wait()
        return carry

    lax.fori_loop(0, CHUNKS, arrived, 0)


def move_kernel(mixed_in, r_in, precond_in, mixed_ref, r_ref, precond_ref, sem):
    pairs = [(mixed_in, mixed_ref), (precond_in, precond_ref), (r_in, r_ref)]
    copies = [pltpu.make_async_copy(a, b, sem.at[i]) for i, (a, b) in enumerate(pairs)]
    for copy in copies:
        copy.start()
    for copy in copies:
        copy.wait()


def body(panel, signs, sample_rows):
    cols, count = panel.shape
    total = count * lax.axis_size("wide") * lax.axis_size("narrow")
    root = math.sqrt(total)
    any_space = pl.BlockSpec(memory_space=pl.ANY)
    vmem = pl.BlockSpec(memory_space=pltpu.VMEM)
    chunked = pltpu.VMEM((CHUNKS, GROUP, count), F32)
    small = pltpu.VMEM((GROUP, 128), F32)
    dma = pltpu.SemaphoreType.DMA
    shapes = [(cols, count), (cols, cols), (cols, count)]
    arguments = (panel, signs.reshape(1, count), sample_rows.reshape(-1, 128))
    results = pl.pallas_call(
        functools.partial(mix_kernel, total / sample_rows.shape[0], root),
        out_shape=tuple(pltpu.VMEM(shape, F32) for shape in shapes),
        in_specs=[any_space] * 3,
        out_specs=(vmem,) * 3,
        scratch_shapes=[
            chunked,
            pltpu.VMEM((1, count), jnp.int32),
            pltpu.VMEM((128, 128), jnp.int32),
            pltpu.VMEM((INNER, INNER), BF16),
        ]
        + [chunked] * 8
        + [
            pltpu.VMEM((4 * cols, count), BF16),
            pltpu.VMEM((128, 128), F32),
            pltpu.VMEM((cols, 128), F32),
            pltpu.VMEM((N_Z, GROUP, 128), F32),
            small,
            pltpu.VMEM((PLANE, GROUP, 128), F32),
            pltpu.VMEM((cols, 128), F32),
            pltpu.VMEM((cols, 128), F32),
        ]
        + [dma((CHUNKS,))] * 2
        + [dma, dma]
        + [dma((CHUNKS,))] * 10
        + [dma((1,))] * 4
        + [dma((2,))] * 2
        + [dma((1,))] * 2
        + [pltpu.SemaphoreType.REGULAR] * 2,
        compiler_params=pltpu.CompilerParams(
            collective_id=0, has_side_effects=True, vmem_limit_bytes=48 * 1024 * 1024
        ),
    )(*(pltpu.with_memory_space_constraint(one, pltpu.HBM) for one in arguments))
    return pl.pallas_call(
        move_kernel,
        out_shape=tuple(jax.ShapeDtypeStruct(shape, F32) for shape in shapes),
        in_specs=[any_space] * 3,
        out_specs=(any_space,) * 3,
        scratch_shapes=[dma((3,))],
        compiler_params=pltpu.CompilerParams(vmem_limit_bytes=1024 * 1024),
    )(*results)


def solution(mesh):
    in_specs = (P(None, ("wide", "narrow")), P(("wide", "narrow")), P())
    out_specs = (P(None, ("wide", "narrow")), P(), P(None, ("wide", "narrow")))
    return jax.shard_map(body, mesh=mesh, in_specs=in_specs, out_specs=out_specs, check_vma=False)
```
